256 devices in a mesh: stretch: 32 (over y_lo, z, core), head: 8 (over y_hi, x).
Axes of the slice: x: 4, y: 4 (y_hi: 2, y_lo: 2; y = y_hi * 2 + y_lo), z: 8, core: 2. Of those that a mesh axis runs over, the one named last changes fastest.
Arguments:
- query_raw: bfloat16 [8192, 5120], P('stretch', 'head'), may hold values from -1000 to 1000
- key_raw: bfloat16 [8192, 5120], P('stretch', 'head'), may hold values from -1000 to 1000
- values: bfloat16 [8192, 5120], P('stretch', 'head'), may hold values from -6 to 6
- query_gain: float32 [5120], P('head'), may hold values from 0.25 to 1.75
- key_gain: float32 [5120], P('head'), may hold values from 0.25 to 1.75
- recent_ids: int32 [32, 2], P('stretch'), may hold values from -1 to 30, as said below
- sink_ids: int32 [32, 1], P('stretch'), may hold values from -1 to 1, as said below
- out_grad: bfloat16 [8192, 5120], P('stretch', 'head'), may hold values from -6 to 6
Outputs:
- attended: bfloat16 [8192, 5120], P('stretch', 'head')
- query_grad: bfloat16 [8192, 5120], P('stretch', 'head')
- key_grad: bfloat16 [8192, 5120], P('stretch', 'head')
- value_grad: bfloat16 [8192, 5120], P('stretch', 'head')
The draws below stay inside these ranges and needn't reach their ends.
Inputs may be any that keep to these rules, and one draw needn't show every extreme that they name: `recent_ids`: row c names the stretch c - 1 first and then one stretch from c - 3 to c - 2; an entry that would lie before stretch 0 is -1. `sink_ids`: row c names one stretch among the first 2 that lies before c, or -1 where none does; it may also stand in the row's recent list. Row c names stretch c - 1 for c from 1 to 2, and the last row names stretch 1.
All inputs are finite; a program needn't handle non-finite values.
Results may differ from the reference program's by a relative error of at most 0.04.
Values may be sent and summed in bfloat16 or wider, within the bound.
A program may use at most 64 MiB of HBM per device.

```python
import math
import jax
import jax.numpy as jnp
from jax import lax

D = 5120
HEADS = 40
HDIM = 128
TOKC = 256
WINDOW = 3
SINK_POOL = 2
STRETCHES = 32


def spread_table(key, span):
    row_key, col_key, base_key = jax.random.split(key, 3)
    count = STRETCHES * TOKC
    row_scale = jnp.exp(jax.random.uniform(row_key, (count, 1), jnp.float32, 0.0, math.log(10.0)))
    ramp = 1.0 + 2.0 * jnp.arange(D, dtype=jnp.float32) / (D - 1)
    col_scale = ramp * jnp.exp(jax.random.uniform(col_key, (D,), jnp.float32, 0.0, math.log(span)))
    return jax.random.normal(base_key, (count, D), jnp.float32) * row_scale * col_scale


def draw_key_raw(key, part):
    shared = spread_table(key, 3.4)
    return jnp.clip(shared, -1000.0, 1000.0).astype(jnp.bfloat16)


def draw_query_raw(key, part):
    key = jax.random.fold_in(key, 13)
    table = spread_table(key, 3.4)
    return jnp.clip(table, -1000.0, 1000.0).astype(jnp.bfloat16)


def draw_recent_ids(key, part):
    key = jax.random.fold_in(key, 21)
    stretch_ids = jnp.arange(STRETCHES, dtype=jnp.int32)
    further = jax.random.randint(key, (STRETCHES,), 2, WINDOW + 1, dtype=jnp.int32)
    first = stretch_ids - 1
    second = stretch_ids - further
    listed = jnp.stack([first, second], axis=1)
    return jnp.where(listed >= 0, listed, -1).astype(jnp.int32)


def draw_sink_ids(key, part):
    key = jax.random.fold_in(key, 33)
    stretch_ids = jnp.arange(STRETCHES, dtype=jnp.int32)
    picked = jax.random.randint(key, (STRETCHES,), 0, SINK_POOL, dtype=jnp.int32)
    early = (stretch_ids >= 1) & (stretch_ids <= SINK_POOL)
    picked = jnp.where(early, stretch_ids - 1, picked)
    picked = jnp.where(stretch_ids == STRETCHES - 1, SINK_POOL - 1, picked)
    picked = jnp.where(picked < stretch_ids, picked, -1)
    return picked[:, None].astype(jnp.int32)


def level_of(rng, extent, cuts, smallest, high):
    loudness, own = 1.0, jax.random.fold_in(rng, 6)
    for axis_at, shards_of in cuts:
        draws = jnp.exp(jax.random.uniform(jax.random.fold_in(own, axis_at), (shards_of,), jnp.float32, smallest / len(cuts), high / len(cuts)))
        loudness = loudness * jnp.repeat(draws, extent[axis_at] // shards_of).reshape([-1 if axis == axis_at else 1 for axis in range(len(extent))])
    return loudness


def scatter_about(key, dims, scale, bound, cuts=(), kind=jnp.bfloat16):
    drawn = scale * jax.random.normal(key, dims, jnp.float32)
    if cuts:
        drawn = drawn * level_of(key, dims, cuts, -0.22, 0.18)
    return jnp.clip(drawn, -bound, bound).astype(kind)


def setup_inputs(seed: int = 0) -> dict:
    arg_keys = jax.random.split(jax.random.key(seed), 9)
    query_raw = draw_query_raw(jax.random.fold_in(arg_keys[8], 71), 0)
    key_raw = draw_key_raw(jax.random.fold_in(arg_keys[8], 71), 0)
    values = scatter_about(arg_keys[2], (STRETCHES * TOKC, D), 1.0, 6.0, ((0, 32), (1, 8)))
    query_gain = jnp.clip(1.0 + 0.15 * jax.random.normal(arg_keys[3], (D,), jnp.float32), 0.25, 1.75)
    key_gain = jnp.clip(1.0 + 0.15 * jax.random.normal(arg_keys[4], (D,), jnp.float32), 0.25, 1.75)
    recent_ids = draw_recent_ids(jax.random.fold_in(arg_keys[8], 71), 0)
    sink_ids = draw_sink_ids(jax.random.fold_in(arg_keys[8], 71), 0)
    out_grad = scatter_about(arg_keys[7], (STRETCHES * TOKC, D), 1.0, 6.0, ((0, 32), (1, 8)))
    return {"query_raw": query_raw, "key_raw": key_raw, "values": values, "query_gain": query_gain, "key_gain": key_gain, "recent_ids": recent_ids, "sink_ids": sink_ids, "out_grad": out_grad}


EPS = 1e-06

def normalize(raw, gain):
    raw_float = raw.astype(jnp.float32)
    inverse = lax.rsqrt(lax.optimization_barrier(jnp.mean(raw_float * raw_float, axis=1, keepdims=True)) + EPS)
    return ((raw_float * inverse * gain).astype(jnp.bfloat16), inverse)

def norm_back(raw, inverse, gain, grad):
    raw_float = raw.astype(jnp.float32)
    scaled = gain * grad
    inner = lax.optimization_barrier(jnp.sum(scaled * raw_float, axis=1, keepdims=True))
    return (inverse * scaled - raw_float * inverse ** 3 * inner / D).astype(jnp.bfloat16)

def reference(query_raw, key_raw, values, query_gain, key_gain, recent_ids, sink_ids, out_grad):
    query_norm, query_inv = normalize(query_raw, query_gain)
    key_norm, key_inv = normalize(key_raw, key_gain)
    scale = HDIM ** (-0.5)
    query_blocks = query_norm.reshape(STRETCHES, TOKC, HEADS, HDIM)
    key_blocks = key_norm.reshape(STRETCHES, TOKC, HEADS, HDIM)
    value_blocks = values.reshape(STRETCHES, TOKC, HEADS, HDIM)
    grad_blocks = out_grad.reshape(STRETCHES, TOKC, HEADS, HDIM)
    own_ids = jnp.arange(STRETCHES, dtype=jnp.int32)[:, None]
    lists = jnp.concatenate([own_ids, recent_ids.astype(jnp.int32), sink_ids.astype(jnp.int32)], axis=1)
    groups = lists.shape[1]

    def one_stretch(carry, item):
        key_acc, value_acc = carry
        listed, query, grad = item
        valid = listed >= 0
        clipped = jnp.maximum(listed, 0).astype(jnp.int32)
        keys = key_blocks[clipped].astype(jnp.float32)
        value_rows = value_blocks[clipped].astype(jnp.float32)
        query_float = query.astype(jnp.float32)
        grad_float = grad.astype(jnp.float32)
        score = jnp.einsum('qhd,gkhd->hqgk', query_float, keys) * scale
        score = jnp.where(valid[None, None, :, None], score, -jnp.inf)
        top = lax.optimization_barrier(jnp.max(score, axis=(2, 3), keepdims=True))
        log_total = top + jnp.log(lax.optimization_barrier(jnp.sum(jnp.exp(score - top), axis=(2, 3), keepdims=True)))
        prob = jnp.exp(score - log_total)
        weight = prob.astype(jnp.bfloat16).astype(jnp.float32)
        attended = jnp.einsum('hqgk,gkhd->qhd', weight, value_rows).astype(jnp.bfloat16)
        delta = lax.optimization_barrier(jnp.sum(grad_float * attended.astype(jnp.float32), axis=2))
        dprob = jnp.einsum('qhd,gkhd->hqgk', grad_float, value_rows)
        dscore = (prob * (dprob - delta.T[:, :, None, None])).astype(jnp.bfloat16).astype(jnp.float32)
        query_delta = jnp.einsum('hqgk,gkhd->qhd', dscore, keys) * scale
        key_terms = jnp.einsum('hqgk,qhd->gkhd', dscore, query_float) * scale
        value_terms = jnp.einsum('hqgk,qhd->gkhd', weight, grad_float)
        for group in range(groups):
            key_acc = key_acc.at[clipped[group]].add(key_terms[group])
            value_acc = value_acc.at[clipped[group]].add(value_terms[group])
        return ((key_acc, value_acc), (attended, query_delta))
    zeros = jnp.zeros((STRETCHES, TOKC, HEADS, HDIM), jnp.float32)
    (key_acc, value_acc), (attended, query_delta) = lax.scan(one_stretch, (zeros, zeros), (lists, query_blocks, grad_blocks))
    rows = STRETCHES * TOKC
    query_grad = norm_back(query_raw, query_inv, query_gain, query_delta.reshape(rows, D))
    key_grad = norm_back(key_raw, key_inv, key_gain, key_acc.reshape(rows, D))
    value_grad = value_acc.reshape(rows, D).astype(jnp.bfloat16)
    return (attended.reshape(rows, D), query_grad, key_grad, value_grad)
```

```python
import jax
import jax.numpy as jnp
from jax import lax
from jax.experimental import pallas as pl
from jax.experimental.pallas import tpu as pltpu
from jax.sharding import PartitionSpec as P

D = 5120
HDIM = 128
TOKC = 256
HEADS = 5
STRETCHES = 32
HEAD_DEVICES = 8
EPS = 1e-06
SCALE = HDIM ** (-0.5)
SCALE2 = SCALE * 1.4426950408889634
FAR_AWAY = 1e30
MESH = pl.DeviceIdType.MESH
F32 = jnp.float32
BF16 = jnp.bfloat16


def dot_t(a, b):
    return lax.dot_general(a, b, (((1,), (1,)), ((), ())), preferred_element_type=F32)


def dot_n(a, b):
    return lax.dot_general(a, b, (((1,), (0,)), ((), ())), preferred_element_type=F32)


def to_rows(columns):
    lane = lax.broadcasted_iota(jnp.int32, (TOKC, HDIM), 1)
    spread = jnp.zeros((TOKC, HDIM), F32)
    for i, column in enumerate(columns):
        spread = jnp.where(lane == i, column, spread)
    return spread.T[:8]


def to_full(row):
    return jnp.broadcast_to(row, (HDIM, TOKC)).T


def remote(src, dst, send, recv, device):
    return pltpu.make_async_remote_copy(
        src_ref=src, dst_ref=dst, send_sem=send, recv_sem=recv, device_id=device, device_id_type=MESH
    )


def kernel(
    query_hbm, key_hbm, values_hbm, grad_hbm, query_gain, key_gain, recent, sink,
    att_out, dq_out, dk_out, dv_out,
    raw, kv, qd, kvr, qdr, sinkb, red, rr1, rr2, acc, up, dq, dk, dv, stat, statr, tile, tiler, inv,
    load_sem, kvs, kvrs, qds, qdrs, sks, skc, skr, sts, strs, ars, arr, rs1, rr1s, rs2, rr2s,
):
    c = lax.axis_index("stretch")
    g = lax.axis_index("head")
    par = c % 2
    z = (c // 2) % 8
    y = c // 16
    j = y * 2 + par

    def dev(stretch):
        return (stretch % STRETCHES, g)

    partner = (c + 1 - 2 * par, g)
    is_root = c < 2
    nonroot_rep = jnp.logical_and(z >= 1, y == par)
    is_rep = jnp.logical_or(is_root, nonroot_rep)
    parent_z = jnp.where((z == 3) | (z == 4), 2, jnp.where((z == 5) | (z == 6), 7, 0))
    parent = (jnp.where(parent_z == 0, par, 2 * parent_z + 17 * par), g)
    parent_slot = jnp.where((z == 2) | (z == 4) | (z == 5), 1, jnp.where(z == 7, 2, 0))
    rep_j = jnp.where(z == 0, par, 3 * par)

    def member(i):
        at = (rep_j + 1 + i) % 4
        return ((at // 2) * 16 + 2 * z + at % 2, g)

    def child(child_z):
        return (2 * child_z + 17 * par, g)

    children = ((0, (1, 2, 7)), (2, (3, 4)), (7, (6, 5)))

    order = ((0, 0, key_hbm, raw, 1), (1, 1, query_hbm, raw, 0), (2, 2, values_hbm, kv, 0), (3, 3, grad_hbm, qd, 0))

    def load(i, hbm, dst, part, h):
        return pltpu.make_async_copy(
            hbm.at[:, pl.ds(h * HDIM, HDIM)], dst.at[part, h], load_sem.at[i, h]
        )

    for i, _, hbm, dst, part in order:
        for h in range(HEADS):
            load(i, hbm, dst, part, h).start()

    barrier = pltpu.get_barrier_semaphore()

    def greet(device):
        pl.semaphore_signal(barrier, inc=1, device_id=device, device_id_type=MESH)

    for step in (1, 2, 3):
        greet(dev(c + step))
        greet(dev(c - step + STRETCHES))
    greet(dev(c + 16))
    greet(dev(c + 17 - 2 * par))
    for step in range(1, HEAD_DEVICES):
        greet((c, (g + step) % HEAD_DEVICES))

    @pl.when(jnp.logical_and(is_rep, jnp.logical_not(is_root)))
    def _():
        greet(parent)

    for at_z, kids in children:
        @pl.when(jnp.logical_and(is_rep, z == at_z))
        def _():
            for kid in kids:
                greet(child(kid))

    squares = []
    for i, part in ((1, 0), (0, 1)):
        total = jnp.zeros((TOKC, 1), F32)
        for h in range(HEADS):
            load(i, key_hbm, raw, part, h).wait()
            block = raw[part, h].astype(F32)
            total = total + jnp.sum(block * block, axis=1, keepdims=True)
        squares.append(total)
    tile[0] = to_rows(squares)

    edges = jnp.where(z == 0, 3, jnp.where((z == 2) | (z == 7), 2, 0)) + jnp.where(z == 0, 0, 1)
    pl.semaphore_wait(barrier, 15 + jnp.where(is_rep, edges, 0))

    def reduce_copy(phase, step):
        return remote(
            tile.at[phase], tiler.at[phase, step - 1], ars.at[phase, step - 1], arr.at[phase, step - 1],
            (c, (g + step) % HEAD_DEVICES),
        )

    def reduce_start(phase):
        for step in range(1, HEAD_DEVICES):
            reduce_copy(phase, step).start()

    def reduce_finish(phase):
        total = tile[phase]
        for step in range(1, HEAD_DEVICES):
            reduce_copy(phase, step).wait_recv()
            total = total + tiler[phase, step - 1]
        return total

    reduce_start(0)

    def kv_copies(p, h):
        return (
            remote(kv.at[p, h], kvr.at[1, p, h], kvs.at[0, p, h], kvrs.at[1, p, h], dev(c + 2)),
            remote(
                kv.at[p, h], kvr.at[2 * par, p, h], kvs.at[1, p, h], kvrs.at[2 * par, p, h],
                dev(c + 1 + 2 * par),
            ),
        )

    def qd_copies(p, h):
        return (
            remote(qd.at[p, h], qdr.at[1, p, h], qds.at[0, p, h], qdrs.at[1, p, h], dev(c + STRETCHES - 2)),
            remote(
                qd.at[p, h], qdr.at[2 - 2 * par, p, h], qds.at[1, p, h], qdrs.at[2 - 2 * par, p, h],
                dev(c + STRETCHES - 3 + 2 * par),
            ),
        )

    def kv_forward(p, h):
        return remote(
            kvr.at[1, p, h], kvr.at[2 - 2 * par, p, h], kvs.at[2, p, h], kvrs.at[2 - 2 * par, p, h], partner
        )

    def qd_forward(p, h):
        return remote(
            qdr.at[1, p, h], qdr.at[2 * par, p, h], qds.at[2, p, h], qdrs.at[2 * par, p, h], partner
        )

    def kv_arrived(slot, p, h):
        remote(kvr.at[slot, p, h], kvr.at[slot, p, h], kvs.at[0, p, h], kvrs.at[slot, p, h], partner).wait_recv()

    def qd_arrived(slot, p, h):
        remote(qdr.at[slot, p, h], qdr.at[slot, p, h], qds.at[0, p, h], qdrs.at[slot, p, h], partner).wait_recv()

    def sink_arrived(s, p, h):
        remote(sinkb.at[s, p, h], sinkb.at[s, p, h], sks.at[0, p, h], skr.at[s, p, h], partner).wait_recv()

    def member_copy(i, p, h):
        return remote(sinkb.at[par, p, h], sinkb.at[par, p, h], sks.at[i, p, h], skr.at[par, p, h], member(i))

    def child_copy(i, kid, p, h):
        return remote(sinkb.at[par, p, h], sinkb.at[par, p, h], skc.at[i, p, h], skr.at[par, p, h], child(kid))

    def sink_send(p, h):
        for at_z, kids in children:
            @pl.when(z == at_z)
            def _():
                for i, kid in enumerate(kids):
                    child_copy(i, kid, p, h).start()

        for i in range(3):
            member_copy(i, p, h).start()

    def send(p, h):
        @pl.when(is_root)
        def _():
            sinkb[par, p, h] = kv[p, h]
            sink_send(p, h)

        for copy in kv_copies(p, h) + qd_copies(p, h):
            copy.start()

    def forward(p, h):
        @pl.when(nonroot_rep)
        def _():
            sink_arrived(par, p, h)
            sink_send(p, h)

        kv_arrived(1, p, h)
        kv_forward(p, h).start()
        qd_arrived(1, p, h)
        qd_forward(p, h).start()

    def loop(count, body):
        lax.fori_loop(0, count, lambda h, _: (body(h), 0)[1], 0)

    for h in range(HEADS):
        load(2, values_hbm, kv, 0, h).wait()
        load(3, grad_hbm, qd, 0, h).wait()
    loop(HEADS, lambda h: send(0, h))

    inverse = lax.rsqrt(reduce_finish(0) / D + EPS)
    inv[0] = to_full(inverse[0:1])
    inv[1] = to_full(inverse[1:2])

    def normalize(h):
        qd[1, h] = (raw[0, h].astype(F32) * inv[0] * query_gain[h]).astype(BF16)
        kv[1, h] = (raw[1, h].astype(F32) * inv[1] * key_gain[h]).astype(BF16)
        send(1, h)

    loop(HEADS, normalize)
    loop(HEADS, lambda h: forward(0, h))

    far = recent[0, 1]
    sink_id = sink[0, 0]
    far_two = jnp.logical_and(far == c - 2, c >= 2)
    far_three = jnp.logical_and(far == c - 3, c >= 3)
    two = jnp.where(far_two, 1.0, 0.0).astype(F32)
    sink_one = jnp.where(sink_id == 1, 1.0, 0.0).astype(F32)
    sink_zero = jnp.where(sink_id == 0, 1.0, 0.0).astype(F32)
    near_off = jnp.where(c >= 1, 0.0, FAR_AWAY).astype(F32)
    two_off = jnp.where(far_two, 0.0, FAR_AWAY).astype(F32)
    three_off = jnp.where(far_three, 0.0, FAR_AWAY).astype(F32)
    far_off = jnp.minimum(two_off, three_off)
    sink_off = jnp.where(sink_id >= 0, 0.0, FAR_AWAY).astype(F32)

    def mix(first, second, share):
        return (first.astype(F32) * share + second.astype(F32) * (1.0 - share)).astype(BF16)

    def key_side(keys, vals, queries, grads, log_row, delta_row):
        prob = jnp.exp2(dot_t(keys, queries) * SCALE2 - log_row)
        dprob = dot_t(vals, grads)
        dscore = (prob * (dprob - delta_row)).astype(BF16)
        return dot_n(dscore, queries), dot_n(prob.astype(BF16), grads)

    def stat_copy(step, h):
        return remote(
            stat.at[h], statr.at[step - 1, h], sts.at[step - 1, h], strs.at[step - 1, h], dev(c + STRETCHES - step)
        )

    def rep_of(s):
        return 2 * z if s == 0 else jnp.where(z == 0, 1, 2 * z + 17)

    def rep_at(s):
        return 0 if s == 0 else jnp.where(z == 0, 1, 3)

    def partial_copy(s, h):
        slot = (j - rep_at(s) + 3) % 4
        return remote(
            red.at[s, h], rr1.at[slot, h], rs1.at[s, h], rr1s.at[slot, h], (rep_of(s), g)
        )

    def query_side(h):
        for p in (0, 1):
            kv_arrived(0, p, h)
            kv_arrived(2, p, h)
            sink_arrived(1 - par, p, h)

            @pl.when(jnp.logical_not(is_rep))
            def _():
                sink_arrived(par, p, h)

        queries, grads = qd[1, h], qd[0, h]
        sink_keys = mix(sinkb[1, 1, h], sinkb[0, 1, h], sink_one)
        sink_vals = mix(sinkb[1, 0, h], sinkb[0, 0, h], sink_one)
        blocks = (
            (kv[1, h], kv[0, h], 0.0),
            (kvr[0, 1, h], kvr[0, 0, h], near_off),
            (mix(kvr[1, 1, h], kvr[2, 1, h], two), mix(kvr[1, 0, h], kvr[2, 0, h], two), far_off),
            (sink_keys, sink_vals, sink_off),
        )
        scores = [dot_t(queries, keys) * SCALE2 for keys, _, _ in blocks]
        top = None
        for score, block in zip(scores, blocks):
            here = jnp.max(score, axis=1, keepdims=True) - block[2]
            top = here if top is None else jnp.maximum(top, here)
        probs = [jnp.exp2(score - (top + block[2])) for score, block in zip(scores, blocks)]
        total = None
        for prob in probs:
            here = jnp.sum(prob, axis=1, keepdims=True)
            total = here if total is None else total + here
        share = 1.0 / total
        attended = jnp.zeros((TOKC, HDIM), F32)
        probs = [prob * share for prob in probs]
        for prob, block in zip(probs, blocks):
            attended = attended + dot_n(prob.astype(BF16), block[1])
        attended = attended.astype(BF16)
        att_out[:, pl.ds(pl.multiple_of(h * HDIM, HDIM), HDIM)] = attended
        delta = jnp.sum(grads.astype(F32) * attended.astype(F32), axis=1, keepdims=True)
        log_total = top + jnp.log2(total)
        rows = to_rows(
            (
                log_total, delta, log_total + near_off, log_total + two_off, log_total + three_off,
                log_total + sink_off,
            )
        )
        stat[h] = rows
        for step in (1, 2, 3):
            stat_copy(step, h).start()
        sink_dk, sink_dv = key_side(sink_keys, sink_vals, queries, grads, rows[5:6], rows[1:2])
        for s, mine in ((0, sink_zero), (1, sink_one)):
            red[s, h, 0] = (sink_dk * mine).astype(BF16)
            red[s, h, 1] = (sink_dv * mine).astype(BF16)

            @pl.when(c != rep_of(s))
            def _():
                partial_copy(s, h).start()

        query_delta = jnp.zeros((TOKC, HDIM), F32)
        for prob, block in zip(probs, blocks):
            dscore = (prob * (dot_t(grads, block[1]) - delta)).astype(BF16)
            query_delta = query_delta + dot_n(dscore, block[0])
        dq[h] = query_delta * SCALE

    def owner_side(h):
        keys, vals = kv[1, h], kv[0, h]
        key_sum, value_sum = key_side(keys, vals, qd[1, h], qd[0, h], stat[h, 0:1], stat[h, 1:2])
        for slot in range(3):
            for p in (0, 1):
                if slot != 1:
                    qd_arrived(slot, p, h)
            stat_copy(slot + 1, h).wait_recv()
            more_keys, more_values = key_side(
                keys, vals, qdr[slot, 1, h], qdr[slot, 0, h],
                statr[slot, h, slot + 2:slot + 3], statr[slot, h, 1:2],
            )
            key_sum, value_sum = key_sum + more_keys, value_sum + more_values
        dk[h] = key_sum
        dv[h] = value_sum

    def up_copy(h):
        return remote(up.at[h], rr2.at[parent_slot, h], rs2.at[h], rr2s.at[parent_slot, h], parent)

    def plane_sum(h):
        for slot in range(3):
            remote(rr1.at[slot, h], rr1.at[slot, h], rs1.at[0, h], rr1s.at[slot, h], partner).wait_recv()
        for part in (0, 1):
            total = red[par, h, part].astype(F32)
            for slot in range(3):
                total = total + rr1[slot, h, part].astype(F32)
            acc[h, part] = total

        @pl.when(jnp.logical_and(z % 7 != 0, z != 2))
        def _():
            up[h] = acc[h].astype(BF16)
            up_copy(h).start()

    def children_sum(h, count):
        for slot in range(count):
            remote(rr2.at[slot, h], rr2.at[slot, h], rs2.at[h], rr2s.at[slot, h], partner).wait_recv()
        for part in (0, 1):
            total = acc[h, part]
            for slot in range(count):
                total = total + rr2[slot, h, part].astype(F32)
            acc[h, part] = total

    def step(at):
        @pl.when(at < HEADS)
        def _():
            forward(1, at)

        @pl.when(jnp.logical_and(at >= 1, at <= HEADS))
        def _():
            query_side(at - 1)

        @pl.when(jnp.logical_and(at >= 2, at <= HEADS + 1))
        def _():
            owner_side(at - 2)

            @pl.when(is_rep)
            def _():
                plane_sum(at - 2)

        @pl.when(jnp.logical_and(at >= 3, at <= HEADS + 2))
        def _():
            @pl.when(jnp.logical_and(nonroot_rep, jnp.logical_or(z == 2, z == 7)))
            def _():
                children_sum(at - 3, 2)
                up[at - 3] = acc[at - 3].astype(BF16)
                up_copy(at - 3).start()

        @pl.when(jnp.logical_and(at >= 4, at <= HEADS + 3))
        def _():
            @pl.when(is_root)
            def _():
                children_sum(at - 4, 3)
                dk[at - 4] = dk[at - 4] + acc[at - 4, 0]
                dv[at - 4] = dv[at - 4] + acc[at - 4, 1]

    loop(HEADS + 4, step)

    def inner(h, sums):
        query_sum, key_sum = sums
        query_sum = query_sum + jnp.sum(
            dq[h] * query_gain[h] * raw[0, h].astype(F32), axis=1, keepdims=True
        )
        key_sum = key_sum + jnp.sum(
            dk[h] * SCALE * key_gain[h] * raw[1, h].astype(F32), axis=1, keepdims=True
        )
        return query_sum, key_sum

    zero = jnp.zeros((TOKC, 1), F32)
    tile[1] = to_rows(lax.fori_loop(0, HEADS, inner, (zero, zero)))
    reduce_start(1)
    total = reduce_finish(1)
    query_inner = to_full(total[0:1]) * inv[0] * inv[0] * inv[0] / D
    key_inner = to_full(total[1:2]) * inv[1] * inv[1] * inv[1] / D
    tiler[1, 0] = total
    for h in range(HEADS):
        at = pl.ds(h * HDIM, HDIM)
        dq_out[:, at] = (
            dq[h] * query_gain[h] * inv[0] - raw[0, h].astype(F32) * query_inner
        ).astype(BF16)
        dk_out[:, at] = (
            dk[h] * SCALE * key_gain[h] * inv[1] - raw[1, h].astype(F32) * key_inner
        ).astype(BF16)
        dv_out[:, at] = dv[h].astype(BF16)

    def drain(h):
        for p in (0, 1):
            for copy in kv_copies(p, h) + qd_copies(p, h):
                copy.wait_send()
            kv_forward(p, h).wait_send()
            qd_forward(p, h).wait_send()

            @pl.when(is_rep)
            def _():
                for at_z, kids in children:
                    @pl.when(z == at_z)
                    def _():
                        for i, kid in enumerate(kids):
                            child_copy(i, kid, p, h).wait_send()

                for i in range(3):
                    member_copy(i, p, h).wait_send()

        for step in (1, 2, 3):
            stat_copy(step, h).wait_send()
        for s in (0, 1):
            @pl.when(c != rep_of(s))
            def _():
                partial_copy(s, h).wait_send()

        @pl.when(nonroot_rep)
        def _():
            up_copy(h).wait_send()

    loop(HEADS, drain)
    for phase in (0, 1):
        for step in range(1, HEAD_DEVICES):
            reduce_copy(phase, step).wait_send()


def per_device(query_raw, key_raw, values, query_gain, key_gain, recent_ids, sink_ids, out_grad):
    rows, width = query_raw.shape
    block = (HEADS, TOKC, HDIM)
    dma = pltpu.SemaphoreType.DMA
    any_spec = pl.BlockSpec(memory_space=pl.ANY)
    vmem = pl.BlockSpec(memory_space=pltpu.VMEM)
    smem = pl.BlockSpec(memory_space=pltpu.SMEM)
    return pl.pallas_call(
        kernel,
        out_shape=[jax.ShapeDtypeStruct((rows, width), BF16)] * 4,
        in_specs=[any_spec] * 4 + [vmem] * 2 + [smem] * 2,
        out_specs=[vmem] * 4,
        scratch_shapes=[
            pltpu.VMEM((2,) + block, BF16),
            pltpu.VMEM((2,) + block, BF16),
            pltpu.VMEM((2,) + block, BF16),
            pltpu.VMEM((3, 2) + block, BF16),
            pltpu.VMEM((3, 2) + block, BF16),
            pltpu.VMEM((2, 2) + block, BF16),
            pltpu.VMEM((2, HEADS, 2, TOKC, HDIM), BF16),
            pltpu.VMEM((3, HEADS, 2, TOKC, HDIM), BF16),
            pltpu.VMEM((3, HEADS, 2, TOKC, HDIM), BF16),
            pltpu.VMEM((HEADS, 2, TOKC, HDIM), F32),
            pltpu.VMEM((HEADS, 2, TOKC, HDIM), BF16),
            pltpu.VMEM(block, F32),
            pltpu.VMEM(block, F32),
            pltpu.VMEM(block, F32),
            pltpu.VMEM((HEADS, 8, TOKC), F32),
            pltpu.VMEM((3, HEADS, 8, TOKC), F32),
            pltpu.VMEM((2, 8, TOKC), F32),
            pltpu.VMEM((2, HEAD_DEVICES - 1, 8, TOKC), F32),
            pltpu.VMEM((2, TOKC, HDIM), F32),
            dma((4, HEADS)),
            dma((3, 2, HEADS)),
            dma((3, 2, HEADS)),
            dma((3, 2, HEADS)),
            dma((3, 2, HEADS)),
            dma((3, 2, HEADS)),
            dma((3, 2, HEADS)),
            dma((2, 2, HEADS)),
            dma((3, HEADS)),
            dma((3, HEADS)),
            dma((2, HEAD_DEVICES - 1)),
            dma((2, HEAD_DEVICES - 1)),
            dma((2, HEADS)),
            dma((3, HEADS)),
            dma((HEADS,)),
            dma((3, HEADS)),
        ],
        compiler_params=pltpu.CompilerParams(
            collective_id=0, has_side_effects=True, vmem_limit_bytes=48 * 2**20
        ),
        cost_estimate=pl.CostEstimate(flops=3 * 10**9, bytes_accessed=6 * 10**6, transcendentals=3 * 10**6),
        name="stretch_attention",
    )(
        query_raw, key_raw, values, out_grad,
        query_gain.reshape(HEADS, 1, HDIM), key_gain.reshape(HEADS, 1, HDIM),
        recent_ids, sink_ids,
    )


def solution(mesh):
    split = P("stretch", "head")
    return jax.shard_map(
        per_device,
        mesh=mesh,
        in_specs=(split, split, split, P("head"), P("head"), P("stretch", None), P("stretch", None), split),
        out_specs=(split,) * 4,
        check_vma=False,
    )
```

```python
import jax
import jax.numpy as jnp
from jax import lax
from jax.experimental import pallas as pl
from jax.experimental.pallas import tpu as pltpu
from jax.sharding import PartitionSpec as P

D = 5120
HDIM = 128
TOKC = 256
HEADS = 5
STRETCHES = 32
HEAD_DEVICES = 8
EPS = 1e-06
SCALE = HDIM ** (-0.5)
SCALE2 = SCALE * 1.4426950408889634
FAR_AWAY = 1e30
MESH = pl.DeviceIdType.MESH
NEAR = (1, 2, 3, -1, -2, -3)
KIDS = ({0: (1, 7), 1: (2,), 7: (6, 5), 5: (4, 3)}, {1: (2,), 7: (6, 5, 0), 5: (4, 3)})
VALUE_KIDS = (1, 7)
AHEAD = 2
SUMS = {0: (1, 7, 5), 1: (2,), 7: (6,), 5: (4, 3)}
F32 = jnp.float32
BF16 = jnp.bfloat16


def dot_t(a, b):
    return lax.dot_general(a, b, (((1,), (1,)), ((), ())), preferred_element_type=F32)


def dot_n(a, b):
    return lax.dot_general(a, b, (((1,), (0,)), ((), ())), preferred_element_type=F32)


def to_rows(columns):
    lane = lax.broadcasted_iota(jnp.int32, (TOKC, HDIM), 1)
    spread = jnp.zeros((TOKC, HDIM), F32)
    for i, column in enumerate(columns):
        spread = jnp.where(lane == i, column, spread)
    return spread.T[:8]


def to_full(row):
    return jnp.broadcast_to(row, (HDIM, TOKC)).T


def remote(src, dst, send, recv, device):
    return pltpu.make_async_remote_copy(
        src_ref=src, dst_ref=dst, send_sem=send, recv_sem=recv, device_id=device, device_id_type=MESH
    )


def kernel(
    query_hbm, key_hbm, values_hbm, grad_hbm, query_gain_hbm, key_gain_hbm, recent, sink,
    att_out, dq_out, dk_out, dv_out,
    kv, qd, keyn, queryn, kvr, qdr, sinkb, red, rr1, rr2, acc, up, vin, dq, dk, dv, stat, statr, tile, tiler, inv, gains, sinv, ninv, tsum, tout, tin,
    load_sem, gain_sem, kvs, kvrs, qds, qdrs, sks, skc, skr, sts, strs, ars, arr, rs1, rr1s, rs2, rr2s, vis, vir, crs, svs, svr, tis, tir, nis, nir,
):
    c = lax.axis_index("stretch")
    g = lax.axis_index("head")
    par = c % 2
    z = (c // 2) % 8
    y = c // 16
    part = 1 - y
    even = par == 0
    odd = par == 1
    owner = c < 2
    partner = (c + 1 - 2 * par, g)

    def dev(stretch):
        return (stretch % STRETCHES, g)

    def member(i):
        return (((y + i // 2) % 2) * 16 + 2 * z + (par + i % 2) % 2, g)

    def at_plane(other):
        return (y * 16 + 2 * other + par, g)

    loads = ((values_hbm, kv, 0), (key_hbm, kv, 1), (query_hbm, qd, 1), (grad_hbm, qd, 0))
    level = jnp.where((z == 1) | (z == 7), 1, jnp.where((z == 4) | (z == 3), 3, 2))
    level = jnp.where(owner, 0, level)
    lag_pass = jnp.where(owner, 0, 2 * level - 2)
    lag_relay = 2 * level
    lag_query = jnp.where(owner, 2, 2 * level + 1)
    paced = z == 1
    busy = (z == 7) | (z == 5)

    def load(i, h):
        hbm, dst, p = loads[i]
        return pltpu.make_async_copy(hbm.at[:, pl.ds(h * HDIM, HDIM)], dst.at[h, p], load_sem.at[i, h])

    def load_gain(i, hbm):
        return pltpu.make_async_copy(hbm, gains.at[i], gain_sem.at[i])

    for i in (1, 2, 0, 3):
        for h in range(HEADS):
            load(i, h).start()
    load_gain(0, query_gain_hbm).start()
    load_gain(1, key_gain_hbm).start()

    for missing, buffer, slot in (
        (c == 0, kvr, 0), (c < 2, kvr, 1), (c < 3, kvr, 2), (c > 30, qdr, 0), (c > 29, qdr, 1), (c > 28, qdr, 2),
    ):
        @pl.when(missing)
        def _():
            buffer[slot] = jnp.zeros((HEADS, 2, TOKC, HDIM), BF16)

    barrier = pltpu.get_barrier_semaphore()

    def greet(device):
        pl.semaphore_signal(barrier, inc=1, device_id=device, device_id_type=MESH)

    for shift in (1, 2, 3):
        greet(dev(c + shift))
        greet(dev(c - shift + STRETCHES))
    for i in (1, 2, 3):
        greet(member(i))
    for shift in range(1, HEAD_DEVICES):
        greet((c, (g + shift) % HEAD_DEVICES))

    def greet_all(i, _):
        @pl.when(i != c)
        def _():
            greet((i, g))

        return 0

    @pl.when(owner)
    def _():
        lax.fori_loop(0, STRETCHES, greet_all, 0)

    for root in (0, 1):
        @pl.when(c != root)
        def _():
            greet((root, g))

    degree = jnp.where(owner, STRETCHES, 2)
    for at_z in range(8):
        friends = sorted(set(KIDS[0].get(at_z, ()) + SUMS.get(at_z, ()) + tuple(
            top for table in (KIDS[0], SUMS) for top, below in table.items() if at_z in below)))
        degree = degree + jnp.where(z == at_z, len(friends), 0)

        @pl.when(z == at_z)
        def _():
            for friend in friends:
                greet(at_plane(friend))

    for h in range(HEADS):
        for i in (1, 2, 0, 3):
            load(i, h).wait()

    def square(block):
        block = block.astype(F32)
        return block * block

    def squares(h, sums):
        return sums[0] + square(qd[h, 1]), sums[1] + square(kv[h, 1])

    zeros = jnp.zeros((TOKC, HDIM), F32)
    sums = lax.fori_loop(0, HEADS, squares, (zeros, zeros))
    tile[0] = to_rows([jnp.sum(part_sum, axis=1, keepdims=True) for part_sum in sums])
    pl.semaphore_wait(barrier, 16 + degree)

    def reduce_copy(phase, shift):
        return remote(
            tile.at[phase], tiler.at[phase, shift - 1], ars.at[phase, shift - 1], arr.at[phase, shift - 1],
            (c, (g + shift) % HEAD_DEVICES),
        )

    def reduce_start(phase):
        for shift in range(1, HEAD_DEVICES):
            reduce_copy(phase, shift).start()

    def reduce_finish(phase):
        total = tile[phase]
        for shift in range(1, HEAD_DEVICES):
            reduce_copy(phase, shift).wait_recv()
            total = total + tiler[phase, shift - 1]
        return total

    def kv_own(h):
        return remote(kv.at[h], kvr.at[1, h], kvs.at[0, h], kvrs.at[1, h], dev(c + 2))

    def kv_beside(h):
        return remote(kv.at[h], kvr.at[0, h], kvs.at[1, h], kvrs.at[0, h], dev(c + 1))

    def kv_onward(h):
        return remote(kvr.at[1, h], kvr.at[2, h], kvs.at[1, h], kvrs.at[2, h], dev(c + 1))

    def kv_across(h):
        slot = 2 - 2 * par
        return remote(kvr.at[1, h], kvr.at[slot, h], kvs.at[2, h], kvrs.at[slot, h], partner)

    def qd_own(h):
        return remote(qd.at[h], qdr.at[1, h], qds.at[0, h], qdrs.at[1, h], dev(c + STRETCHES - 2))

    def qd_beside(h):
        return remote(qd.at[h], qdr.at[0, h], qds.at[1, h], qdrs.at[0, h], dev(c + STRETCHES - 1))

    def qd_onward(h):
        return remote(qdr.at[1, h], qdr.at[2, h], qds.at[1, h], qdrs.at[2, h], dev(c + STRETCHES - 1))

    def qd_across(h):
        slot = 2 * par
        return remote(qdr.at[1, h], qdr.at[slot, h], qds.at[2, h], qdrs.at[slot, h], partner)

    def kv_arrived(slot, h):
        remote(kvr.at[slot, h], kvr.at[slot, h], kvs.at[0, h], kvrs.at[slot, h], partner).wait_recv()

    def qd_arrived(slot, h):
        remote(qdr.at[slot, h], qdr.at[slot, h], qds.at[0, h], qdrs.at[slot, h], partner).wait_recv()

    def gate(*steps):
        for condition, action in steps:
            pl.when(condition)(lambda act=action: (act(), None)[1])

    kv_has, qd_has = c >= 2, c <= 29
    kv_on = jnp.logical_and(odd, jnp.logical_and(c >= 3, c <= 29))
    qd_on = jnp.logical_and(even, jnp.logical_and(c >= 2, c <= 28))

    def kv_send(h):
        gate((c <= 29, kv_own(h).start), (even, kv_beside(h).start))

    def kv_forward(h):
        gate((kv_has, lambda: kv_arrived(1, h)), (kv_on, kv_onward(h).start), (kv_has, kv_across(h).start))

    def qd_send(h):
        gate((c >= 2, qd_own(h).start), (odd, qd_beside(h).start))

    def qd_forward(h):
        gate((qd_has, lambda: qd_arrived(1, h)), (qd_on, qd_onward(h).start), (qd_has, qd_across(h).start))

    def sink_arrived(s, p, h):
        remote(sinkb.at[s, p, h], sinkb.at[s, p, h], sks.at[0, h], skr.at[s, p, h], partner).wait_recv()

    def chip_copy(h):
        block = sinkb.at[par, part, h]
        return remote(block, block, sks.at[0, h], skr.at[par, part, h], partner)

    def mate_copy(h):
        block = sinkb.at[par, part, h]
        return remote(block, block, sks.at[1, h], skr.at[par, part, h], member(2))

    def relay_copy(h):
        block = sinkb.at[par, y, h]
        return remote(block, block, sks.at[2, h], skr.at[par, y, h], partner)

    def kid_copy(i, kid, h):
        block = sinkb.at[par, part, h]
        return remote(block, block, skc.at[i, h], skr.at[par, part, h], at_plane(kid))

    def value_copy(i, h):
        block = sinkb.at[par, 0, h]
        return remote(block, block, crs.at[i, h], skr.at[par, 0, h], (16 + 2 * VALUE_KIDS[i] + par, g))

    def each_kid(body):
        for column, table in enumerate(KIDS):
            for at_z, kids in table.items():
                @pl.when(jnp.logical_and(y == column, z == at_z))
                def _():
                    for i, kid in enumerate(kids):
                        body(i, kid)

    has_mate = jnp.logical_or(y == 0, z > 0)

    def sink_send(h):
        each_kid(lambda i, kid: kid_copy(i, kid, h).start())
        gate((has_mate, mate_copy(h).start))
        chip_copy(h).start()

    def sink_pass(h):
        @pl.when(jnp.logical_not(owner))
        def _():
            sink_arrived(par, part, h)
            sink_send(h)

    def sink_relay(h):
        @pl.when(jnp.logical_not(owner))
        def _():
            sink_arrived(par, y, h)
            relay_copy(h).start()

    def inverse_copy(stretch):
        return remote(stat_inv, sinv.at[par], svs.at[stretch], svr.at[par], (stretch, g))

    def inverse_arrived(s):
        remote(sinv.at[s], sinv.at[s], svs.at[0], svr.at[s], partner).wait_recv()

    stat_inv = sinv.at[2]

    def each_other(body):
        def at(i, _):
            @pl.when(i != c)
            def _():
                body(i)

            return 0

        lax.fori_loop(0, STRETCHES, at, 0)

    def loop(count, step):
        lax.fori_loop(0, count, lambda h, _: (step(h), 0)[1], 0)

    def launch(h):
        @pl.when(owner)
        def _():
            for p in (0, 1):
                sinkb[par, p, h] = kv[h, p]
            for i in range(len(VALUE_KIDS)):
                value_copy(i, h).start()
            sink_send(h)
            relay_copy(h).start()

        gate((jnp.logical_or(h < AHEAD, jnp.logical_not(paced)), lambda: kv_send(h)))

    def loop_from(low, high, step):
        lax.fori_loop(low, high, lambda h, _: (step(h), 0)[1], 0)

    reduce_start(0)
    loop_from(0, AHEAD, launch)

    for i, hbm in enumerate((query_gain_hbm, key_gain_hbm)):
        load_gain(i, hbm).wait()
    inverse = lax.rsqrt(reduce_finish(0) / D + EPS)
    sinv[2] = inverse

    @pl.when(owner)
    def _():
        sinv[par] = inverse
        each_other(lambda i: inverse_copy(i).start())

    def near_copy(i):
        shift = NEAR[i]
        return remote(sinv.at[2], ninv.at[i], nis.at[i], nir.at[i], dev(c + STRETCHES + shift))

    for i in range(len(NEAR)):
        near_copy(i).start()
    loop_from(AHEAD, HEADS, launch)
    loop(HEADS, lambda h: gate((jnp.logical_not(busy), lambda: qd_send(h))))
    inv[0] = to_full(inverse[0:1])
    inv[1] = to_full(inverse[1:2])

    def gain(i, h):
        return gains[i, pl.ds(pl.multiple_of(h * HDIM, HDIM), HDIM)].reshape(1, HDIM)

    def normed(block, full, i, h):
        return (block.astype(F32) * full * gain(i, h)).astype(BF16)

    def norms(h):
        queryn[h] = normed(qd[h, 1], inv[0], 0, h)
        keyn[h] = normed(kv[h, 1], inv[1], 1, h)

    loop(HEADS, norms)

    far = recent[0, 1]
    sink_id = sink[0, 0]
    far_two = jnp.logical_and(far == c - 2, c >= 2)
    far_three = jnp.logical_and(far == c - 3, c >= 3)
    two = jnp.where(far_two, 1.0, 0.0).astype(F32)
    sink_one = jnp.where(sink_id == 1, 1.0, 0.0).astype(F32)
    sink_zero = jnp.where(sink_id == 0, 1.0, 0.0).astype(F32)
    near_off = jnp.where(c >= 1, 0.0, FAR_AWAY).astype(F32)
    two_off = jnp.where(far_two, 0.0, FAR_AWAY).astype(F32)
    three_off = jnp.where(far_three, 0.0, FAR_AWAY).astype(F32)
    far_off = jnp.minimum(two_off, three_off)
    sink_off = jnp.where(sink_id >= 0, 0.0, FAR_AWAY).astype(F32)

    def blend(first, second, share):
        return first.astype(F32) * share + second.astype(F32) * (1.0 - share)

    def mix(first, second, share):
        return blend(first, second, share).astype(BF16)

    def key_side(keys, vals, queries, grads, log_row, delta_row):
        prob = jnp.exp2(dot_t(keys, queries) * SCALE2 - log_row)
        dprob = dot_t(vals, grads)
        dscore = (prob * (dprob - delta_row)).astype(BF16)
        return dot_n(dscore, queries), dot_n(prob.astype(BF16), grads)

    def stat_copy(shift, h):
        return remote(
            stat.at[h], statr.at[shift - 1, h], sts.at[shift - 1, h], strs.at[shift - 1, h],
            dev(c + STRETCHES - shift),
        )

    def partial_copy(i, h):
        s, p = (par + i % 2) % 2, 1 - (y + i // 2) % 2
        return remote(red.at[s, p, h], rr1.at[i - 1, h], rs1.at[i - 1, h], rr1s.at[i - 1, h], member(i))

    def query_side(h):
        gate((c >= 1, lambda: kv_arrived(0, h)), (c >= 3, lambda: kv_arrived(2, h)))
        for p in (0, 1):
            sink_arrived(1 - par, p, h)

        queries, grads = queryn[h], qd[h, 0]
        sink_raw = blend(sinkb[1, 1, h], sinkb[0, 1, h], sink_one) * gain(1, h)
        sink_keys = (sink_raw * inv[2]).astype(BF16)
        sink_vals = mix(sinkb[1, 0, h], sinkb[0, 0, h], sink_one)
        far_keys = normed(blend(kvr[1, h, 1], kvr[2, h, 1], two), inv[4], 1, h)
        blocks = (
            (keyn[h], kv[h, 0], 0.0),
            (normed(kvr[0, h, 1], inv[3], 1, h), kvr[0, h, 0], near_off),
            (far_keys, mix(kvr[1, h, 0], kvr[2, h, 0], two), far_off),
            (sink_keys, sink_vals, sink_off),
        )
        scores = [dot_t(queries, keys) * SCALE2 for keys, _, _ in blocks]
        top = None
        for score, block in zip(scores, blocks):
            here = jnp.max(score, axis=1, keepdims=True) - block[2]
            top = here if top is None else jnp.maximum(top, here)
        probs = [jnp.exp2(score - (top + block[2])) for score, block in zip(scores, blocks)]
        total = None
        for prob in probs:
            here = jnp.sum(prob, axis=1, keepdims=True)
            total = here if total is None else total + here
        share = 1.0 / total
        attended = jnp.zeros((TOKC, HDIM), F32)
        probs = [prob * share for prob in probs]
        for prob, block in zip(probs, blocks):
            attended = attended + dot_n(prob.astype(BF16), block[1])
        attended = attended.astype(BF16)
        att_out[:, pl.ds(pl.multiple_of(h * HDIM, HDIM), HDIM)] = attended
        delta = jnp.sum(grads.astype(F32) * attended.astype(F32), axis=1, keepdims=True)
        log_total = top + jnp.log2(total)
        rows = to_rows(
            (
                log_total, delta, log_total + near_off, log_total + two_off, log_total + three_off,
                log_total + sink_off,
            )
        )
        stat[h] = rows
        sink_dk, sink_dv = key_side(sink_keys, sink_vals, queries, grads, rows[5:6], rows[1:2])
        tsum[...] = tsum[...] + sink_dk * sink_raw
        for s, mine in ((0, sink_zero), (1, sink_one)):
            red[s, 1, h] = (sink_dk * mine).astype(BF16)
            red[s, 0, h] = (sink_dv * mine).astype(BF16)
        for i in (2, 3, 1):
            partial_copy(i, h).start()
        for shift in (1, 2, 3):
            stat_copy(shift, h).start()

        query_delta = jnp.zeros((TOKC, HDIM), F32)
        for prob, block in zip(probs, blocks):
            dscore = (prob * (dot_t(grads, block[1]) - delta)).astype(BF16)
            query_delta = query_delta + dot_n(dscore, block[0])
        dq[h] = query_delta * SCALE

    def owner_side(h):
        keys, vals = keyn[h], kv[h, 0]
        key_sum, value_sum = key_side(keys, vals, queryn[h], qd[h, 0], stat[h, 0:1], stat[h, 1:2])
        for slot in range(3):
            if slot != 1:
                gate((c <= 30 - slot, lambda: qd_arrived(slot, h)))
            stat_copy(slot + 1, h).wait_recv()
            more_keys, more_values = key_side(
                keys, vals, normed(qdr[slot, h, 1], inv[5 + slot], 0, h), qdr[slot, h, 0],
                statr[slot, h, slot + 2:slot + 3], statr[slot, h, 1:2],
            )
            key_sum, value_sum = key_sum + more_keys, value_sum + more_values
        dk[h] = key_sum
        dv[h] = value_sum

    def up_copy(slot, parent, h):
        return remote(up.at[h], rr2.at[slot, h], rs2.at[h], rr2s.at[slot, h], at_plane(parent))

    def each_parent(body):
        for parent, below in SUMS.items():
            for slot, kid in enumerate(below):
                @pl.when(z == kid)
                def _():
                    body(slot, parent)

    def up_send(h):
        up[h] = acc[h].astype(BF16)
        each_parent(lambda slot, parent: up_copy(slot, parent, h).start())

    def plane_sum(h):
        total = red[par, part, h].astype(F32)
        for slot in range(3):
            remote(rr1.at[slot, h], rr1.at[slot, h], rs1.at[0, h], rr1s.at[slot, h], partner).wait_recv()
            total = total + rr1[slot, h].astype(F32)
        acc[h] = total

        @pl.when(is_leaf)
        def _():
            up_send(h)

    def below_sum(h, count):
        total = acc[h]
        for slot in range(count):
            remote(rr2.at[slot, h], rr2.at[slot, h], rs2.at[h], rr2s.at[slot, h], partner).wait_recv()
            total = total + rr2[slot, h].astype(F32)
        acc[h] = total

    def value_back(h):
        return remote(up.at[h], vin.at[h], vis.at[h], vir.at[h], (par, g))

    is_leaf = z < 0
    for at_z in range(1, 8):
        if at_z not in SUMS:
            is_leaf = jnp.logical_or(is_leaf, z == at_z)

    def when_in(at, low, body):
        @pl.when(jnp.logical_and(at >= low, at < low + HEADS))
        def _():
            body(at - low)

    def middle(h):
        for at_z in SUMS:
            if at_z:
                @pl.when(z == at_z)
                def _():
                    below_sum(h, len(SUMS[at_z]))
                    up_send(h)

    def finish(h):
        below_sum(h, len(SUMS[0]))

        @pl.when(y == 0)
        def _():
            dk[h] = dk[h] + acc[h]

        @pl.when(y == 1)
        def _():
            up[h] = acc[h].astype(BF16)
            value_back(h).start()

    def prepare():
        @pl.when(c != 0)
        def _():
            inverse_arrived(0)

        @pl.when(c != 1)
        def _():
            inverse_arrived(1)

        for i in range(len(NEAR)):
            near_copy(i).wait_recv()
        inv[2] = to_full(sinv[1, 1:2] * sink_one + sinv[0, 1:2] * (1.0 - sink_one))
        inv[3] = to_full(ninv[0, 1:2])
        inv[4] = to_full(ninv[1, 1:2] * two + ninv[2, 1:2] * (1.0 - two))
        for slot in range(3):
            inv[5 + slot] = to_full(ninv[3 + slot, 0:1])

    tsum[...] = jnp.zeros((TOKC, HDIM), F32)

    def step(at):
        when_in(at, 0, kv_forward)
        when_in(at, lag_pass, sink_pass)
        gate((jnp.logical_and(paced, at < HEADS - AHEAD), lambda: kv_send(at + AHEAD)))
        when_in(at, lag_relay, sink_relay)
        when_in(at, lag_pass, lambda h: gate((busy, lambda: qd_send(h))))

        @pl.when(at == lag_query)
        def _():
            prepare()

        when_in(at, lag_query, query_side)
        when_in(at, 4, qd_forward)
        when_in(at, 10, owner_side)
        when_in(at, lag_query + 1, plane_sum)
        when_in(at, 9, middle)

    loop(HEADS + 10, step)

    def tile_copy(root):
        return remote(tout, tin.at[c], tis.at[root], tir.at[c], (root, g))

    sink_inner = jnp.sum(tsum[...], axis=1, keepdims=True) * SCALE
    tout[...] = to_rows((sink_inner * sink_zero, sink_inner * sink_one))
    for root in (0, 1):
        @pl.when(c != root)
        def _():
            tile_copy(root).start()

    def inner(h, sums):
        return (
            sums[0] + dq[h] * (gain(0, h) * qd[h, 1].astype(F32)),
            sums[1] + dk[h] * (gain(1, h) * SCALE * kv[h, 1].astype(F32)),
        )

    sums = lax.fori_loop(0, HEADS, inner, (zeros, zeros))
    tile[1] = to_rows([jnp.sum(part_sum, axis=1, keepdims=True) for part_sum in sums])

    @pl.when(owner)
    def _():
        tin[c] = tout[...]

        def gather(i):
            remote(tin.at[i], tin.at[i], tis.at[0], tir.at[i], partner).wait_recv()
            tin[c] = tin[c] + tin[i]

        each_other(gather)
        sums = tin[c]
        mine = jnp.where(odd, 1.0, 0.0).astype(F32)
        row = sums[0:1] * (1.0 - mine) + sums[1:2] * mine
        level = lax.broadcasted_iota(jnp.int32, (8, TOKC), 0)
        tile[1] = tile[1] + jnp.where(level == 1, row, 0.0)

    reduce_start(1)
    total = reduce_finish(1)
    query_inner = to_full(total[0:1]) * inv[0] * inv[0] * inv[0] / D
    inv[2] = to_full(total[1:2]) * inv[1] * inv[1] * inv[1] / D
    for h in range(HEADS):
        at = pl.ds(h * HDIM, HDIM)
        dq_out[:, at] = (dq[h] * gain(0, h) * inv[0] - qd[h, 1].astype(F32) * query_inner).astype(BF16)

    @pl.when(z == 0)
    def _():
        loop(HEADS, finish)

    for h in range(HEADS):
        at = pl.ds(h * HDIM, HDIM)
        dk_out[:, at] = (dk[h] * SCALE * gain(1, h) * inv[1] - kv[h, 1].astype(F32) * inv[2]).astype(BF16)

    @pl.when(owner)
    def _():
        for h in range(HEADS):
            value_back(h).wait_recv()
            dv[h] = dv[h] + vin[h].astype(F32)

    for h in range(HEADS):
        dv_out[:, pl.ds(h * HDIM, HDIM)] = dv[h].astype(BF16)

    def drain(h):
        gate(
            (c <= 29, kv_own(h).wait_send), (jnp.logical_or(even, kv_on), kv_beside(h).wait_send),
            (kv_has, kv_across(h).wait_send), (c >= 2, qd_own(h).wait_send),
            (jnp.logical_or(odd, qd_on), qd_beside(h).wait_send), (qd_has, qd_across(h).wait_send),
            (has_mate, mate_copy(h).wait_send),
        )
        each_kid(lambda i, kid: kid_copy(i, kid, h).wait_send())
        chip_copy(h).wait_send()
        relay_copy(h).wait_send()
        for i in (1, 2, 3):
            partial_copy(i, h).wait_send()
            stat_copy(i, h).wait_send()
        each_parent(lambda slot, parent: up_copy(slot, parent, h).wait_send())

        @pl.when(owner)
        def _():
            for i in range(len(VALUE_KIDS)):
                value_copy(i, h).wait_send()

        @pl.when(jnp.logical_and(z == 0, y == 1))
        def _():
            value_back(h).wait_send()

    loop(HEADS, drain)

    @pl.when(owner)
    def _():
        each_other(lambda i: inverse_copy(i).wait_send())

    for root in (0, 1):
        @pl.when(c != root)
        def _():
            tile_copy(root).wait_send()

    for i in range(len(NEAR)):
        near_copy(i).wait_send()
    for phase in (0, 1):
        for shift in range(1, HEAD_DEVICES):
            reduce_copy(phase, shift).wait_send()


def per_device(query_raw, key_raw, values, query_gain, key_gain, recent_ids, sink_ids, out_grad):
    rows, width = query_raw.shape
    block = (HEADS, TOKC, HDIM)
    pair = (HEADS, 2, TOKC, HDIM)
    dma = pltpu.SemaphoreType.DMA
    any_spec = pl.BlockSpec(memory_space=pl.ANY)
    vmem = pl.BlockSpec(memory_space=pltpu.VMEM)
    smem = pl.BlockSpec(memory_space=pltpu.SMEM)
    return pl.pallas_call(
        kernel,
        out_shape=[jax.ShapeDtypeStruct((rows, width), BF16)] * 4,
        in_specs=[any_spec] * 6 + [smem] * 2,
        out_specs=[vmem] * 4,
        scratch_shapes=[
            pltpu.VMEM(pair, BF16),
            pltpu.VMEM(pair, BF16),
            pltpu.VMEM(block, BF16),
            pltpu.VMEM(block, BF16),
            pltpu.VMEM((3,) + pair, BF16),
            pltpu.VMEM((3,) + pair, BF16),
            pltpu.VMEM((2, 2) + block, BF16),
            pltpu.VMEM((2, 2) + block, BF16),
            pltpu.VMEM((3,) + block, BF16),
            pltpu.VMEM((3,) + block, BF16),
            pltpu.VMEM(block, F32),
            pltpu.VMEM(block, BF16),
            pltpu.VMEM(block, BF16),
            pltpu.VMEM(block, F32),
            pltpu.VMEM(block, F32),
            pltpu.VMEM(block, F32),
            pltpu.VMEM((HEADS, 8, TOKC), F32),
            pltpu.VMEM((3, HEADS, 8, TOKC), F32),
            pltpu.VMEM((2, 8, TOKC), F32),
            pltpu.VMEM((2, HEAD_DEVICES - 1, 8, TOKC), F32),
            pltpu.VMEM((8, TOKC, HDIM), F32),
            pltpu.VMEM((2, width), F32),
            pltpu.VMEM((3, 8, TOKC), F32),
            pltpu.VMEM((len(NEAR), 8, TOKC), F32),
            pltpu.VMEM((TOKC, HDIM), F32),
            pltpu.VMEM((8, TOKC), F32),
            pltpu.VMEM((STRETCHES, 8, TOKC), F32),
            dma((4, HEADS)),
            dma((2,)),
            dma((3, HEADS)),
            dma((3, HEADS)),
            dma((3, HEADS)),
            dma((3, HEADS)),
            dma((3, HEADS)),
            dma((3, HEADS)),
            dma((2, 2, HEADS)),
            dma((3, HEADS)),
            dma((3, HEADS)),
            dma((2, HEAD_DEVICES - 1)),
            dma((2, HEAD_DEVICES - 1)),
            dma((3, HEADS)),
            dma((3, HEADS)),
            dma((HEADS,)),
            dma((3, HEADS)),
            dma((HEADS,)),
            dma((HEADS,)),
            dma((len(VALUE_KIDS), HEADS)),
            dma((STRETCHES,)),
            dma((2,)),
            dma((2,)),
            dma((STRETCHES,)),
            dma((len(NEAR),)),
            dma((len(NEAR),)),
        ],
        compiler_params=pltpu.CompilerParams(
            collective_id=0, has_side_effects=True, vmem_limit_bytes=60 * 2**20
        ),
        cost_estimate=pl.CostEstimate(flops=3 * 10**9, bytes_accessed=6 * 10**6, transcendentals=3 * 10**6),
        name="stretch_attention",
    )(
        query_raw, key_raw, values, out_grad, query_gain, key_gain, recent_ids, sink_ids,
    )


def solution(mesh):
    split = P("stretch", "head")
    return jax.shard_map(
        per_device,
        mesh=mesh,
        in_specs=(split, split, split, P("head"), P("head"), P("stretch", None), P("stretch", None), split),
        out_specs=(split,) * 4,
        check_vma=False,
    )
```

```python
import jax
import jax.numpy as jnp
from jax import lax
from jax.experimental import pallas as pl
from jax.experimental.pallas import tpu as pltpu
from jax.sharding import PartitionSpec as P

D = 5120
HDIM = 128
TOKC = 256
HEADS = 5
STRETCHES = 32
HEAD_DEVICES = 8
EPS = 1e-06
SCALE = HDIM ** (-0.5)
SCALE2 = SCALE * 1.4426950408889634
FAR_AWAY = 1e30
MESH = pl.DeviceIdType.MESH
NEAR = (1, 2, 3, -1, -2, -3)
KIDS = ({0: (1, 7), 1: (2,), 7: (6, 5), 5: (4, 3)}, {1: (2,), 7: (6, 5, 0), 5: (4, 3)})
VALUE_KIDS = (1, 7)
AHEAD = 3
SUMS = {0: (1, 7, 5), 1: (2,), 7: (6,), 5: (4, 3)}
F32 = jnp.float32
BF16 = jnp.bfloat16


def dot_t(a, b):
    return lax.dot_general(a, b, (((1,), (1,)), ((), ())), preferred_element_type=F32)


def dot_n(a, b):
    return lax.dot_general(a, b, (((1,), (0,)), ((), ())), preferred_element_type=F32)


def to_rows(columns):
    lane = lax.broadcasted_iota(jnp.int32, (TOKC, HDIM), 1)
    spread = jnp.zeros((TOKC, HDIM), F32)
    for i, column in enumerate(columns):
        spread = jnp.where(lane == i, column, spread)
    return spread.T[:8]


def to_full(row):
    return jnp.broadcast_to(row, (HDIM, TOKC)).T


def remote(src, dst, send, recv, device):
    return pltpu.make_async_remote_copy(
        src_ref=src, dst_ref=dst, send_sem=send, recv_sem=recv, device_id=device, device_id_type=MESH
    )


def kernel(
    query_hbm, key_hbm, values_hbm, grad_hbm, query_gain_hbm, key_gain_hbm, recent, sink,
    att_out, dq_out, dk_out, dv_out,
    kv, qd, keyn, queryn, kvr, qdr, sinkb, red, rr1, rr2, acc, up, vin, dq, dk, dv, stat, statr, tile, tiler, inv, gains, sinv, ninv, tsum, tout, tin,
    load_sem, gain_sem, kvs, kvrs, qds, qdrs, sks, skc, skr, sts, strs, ars, arr, rs1, rr1s, rs2, rr2s, vis, vir, crs, svs, svr, tis, tir, nis, nir,
):
    c = lax.axis_index("stretch")
    g = lax.axis_index("head")
    par = c % 2
    z = (c // 2) % 8
    y = c // 16
    part = 1 - y
    even = par == 0
    odd = par == 1
    owner = c < 2
    partner = (c + 1 - 2 * par, g)

    def dev(stretch):
        return (stretch % STRETCHES, g)

    def member(i):
        return (((y + i // 2) % 2) * 16 + 2 * z + (par + i % 2) % 2, g)

    def at_plane(other):
        return (y * 16 + 2 * other + par, g)

    loads = ((values_hbm, kv, 0), (key_hbm, kv, 1), (query_hbm, qd, 1), (grad_hbm, qd, 0))
    level = jnp.where((z == 1) | (z == 7), 1, jnp.where((z == 4) | (z == 3), 3, 2))
    level = jnp.where(owner, 0, level)
    lag_pass = jnp.where(owner, 0, 2 * level - 2)
    lag_relay = 2 * level
    lag_query = jnp.where(owner, 2, 2 * level + 1)
    paced = z == 1
    busy = (z == 7) | (z == 5)
    lag_owner = jnp.where(level == 3, 11, 9)

    def load(i, h):
        hbm, dst, p = loads[i]
        return pltpu.make_async_copy(hbm.at[:, pl.ds(h * HDIM, HDIM)], dst.at[h, p], load_sem.at[i, h])

    def load_gain(i, hbm):
        return pltpu.make_async_copy(hbm, gains.at[i], gain_sem.at[i])

    for i in (1, 2, 0, 3):
        for h in range(HEADS):
            load(i, h).start()
    load_gain(0, query_gain_hbm).start()
    load_gain(1, key_gain_hbm).start()

    for missing, buffer, slot in (
        (c == 0, kvr, 0), (c < 2, kvr, 1), (c < 3, kvr, 2), (c > 30, qdr, 0), (c > 29, qdr, 1), (c > 28, qdr, 2),
    ):
        @pl.when(missing)
        def _():
            buffer[slot] = jnp.zeros((HEADS, 2, TOKC, HDIM), BF16)

    barrier = pltpu.get_barrier_semaphore()

    def greet(device):
        pl.semaphore_signal(barrier, inc=1, device_id=device, device_id_type=MESH)

    for shift in (1, 2, 3):
        greet(dev(c + shift))
        greet(dev(c - shift + STRETCHES))
    for i in (1, 2, 3):
        greet(member(i))
    for shift in range(1, HEAD_DEVICES):
        greet((c, (g + shift) % HEAD_DEVICES))

    def greet_all(i, _):
        @pl.when(i != c)
        def _():
            greet((i, g))

        return 0

    @pl.when(owner)
    def _():
        lax.fori_loop(0, STRETCHES, greet_all, 0)

    for root in (0, 1):
        @pl.when(c != root)
        def _():
            greet((root, g))

    degree = jnp.where(owner, STRETCHES, 2)
    for at_z in range(8):
        friends = sorted(set(KIDS[0].get(at_z, ()) + SUMS.get(at_z, ()) + tuple(
            top for table in (KIDS[0], SUMS) for top, below in table.items() if at_z in below)))
        degree = degree + jnp.where(z == at_z, len(friends), 0)

        @pl.when(z == at_z)
        def _():
            for friend in friends:
                greet(at_plane(friend))

    for h in range(HEADS):
        for i in (1, 2, 0, 3):
            load(i, h).wait()

    def square(block):
        block = block.astype(F32)
        return block * block

    def squares(h, sums):
        return sums[0] + square(qd[h, 1]), sums[1] + square(kv[h, 1])

    zeros = jnp.zeros((TOKC, HDIM), F32)
    sums = lax.fori_loop(0, HEADS, squares, (zeros, zeros))
    tile[0] = to_rows([jnp.sum(part_sum, axis=1, keepdims=True) for part_sum in sums])
    pl.semaphore_wait(barrier, 16 + degree)

    def reduce_copy(phase, shift):
        return remote(
            tile.at[phase], tiler.at[phase, shift - 1], ars.at[phase, shift - 1], arr.at[phase, shift - 1],
            (c, (g + shift) % HEAD_DEVICES),
        )

    def reduce_start(phase):
        for shift in range(1, HEAD_DEVICES):
            reduce_copy(phase, shift).start()

    def reduce_finish(phase):
        total = tile[phase]
        for shift in range(1, HEAD_DEVICES):
            reduce_copy(phase, shift).wait_recv()
            total = total + tiler[phase, shift - 1]
        return total

    def kv_own(h):
        return remote(kv.at[h], kvr.at[1, h], kvs.at[0, h], kvrs.at[1, h], dev(c + 2))

    def kv_beside(h):
        return remote(kv.at[h], kvr.at[0, h], kvs.at[1, h], kvrs.at[0, h], dev(c + 1))

    def kv_onward(h):
        return remote(kvr.at[1, h], kvr.at[2, h], kvs.at[1, h], kvrs.at[2, h], dev(c + 1))

    def kv_across(h):
        slot = 2 - 2 * par
        return remote(kvr.at[1, h], kvr.at[slot, h], kvs.at[2, h], kvrs.at[slot, h], partner)

    def qd_own(h):
        return remote(qd.at[h], qdr.at[1, h], qds.at[0, h], qdrs.at[1, h], dev(c + STRETCHES - 2))

    def qd_beside(h):
        return remote(qd.at[h], qdr.at[0, h], qds.at[1, h], qdrs.at[0, h], dev(c + STRETCHES - 1))

    def qd_onward(h):
        return remote(qdr.at[1, h], qdr.at[2, h], qds.at[1, h], qdrs.at[2, h], dev(c + STRETCHES - 1))

    def qd_across(h):
        slot = 2 * par
        return remote(qdr.at[1, h], qdr.at[slot, h], qds.at[2, h], qdrs.at[slot, h], partner)

    def kv_arrived(slot, h):
        remote(kvr.at[slot, h], kvr.at[slot, h], kvs.at[0, h], kvrs.at[slot, h], partner).wait_recv()

    def qd_arrived(slot, h):
        remote(qdr.at[slot, h], qdr.at[slot, h], qds.at[0, h], qdrs.at[slot, h], partner).wait_recv()

    def gate(*steps):
        for condition, action in steps:
            pl.when(condition)(lambda act=action: (act(), None)[1])

    kv_has, qd_has = c >= 2, c <= 29
    kv_on = jnp.logical_and(odd, jnp.logical_and(c >= 3, c <= 29))
    qd_on = jnp.logical_and(even, jnp.logical_and(c >= 2, c <= 28))

    def kv_send(h):
        gate((c <= 29, kv_own(h).start), (even, kv_beside(h).start))

    def kv_forward(h):
        gate((kv_has, lambda: kv_arrived(1, h)), (kv_on, kv_onward(h).start), (kv_has, kv_across(h).start))

    def qd_send(h):
        gate((c >= 2, qd_own(h).start), (odd, qd_beside(h).start))

    def qd_forward(h):
        gate((qd_has, lambda: qd_arrived(1, h)), (qd_on, qd_onward(h).start), (qd_has, qd_across(h).start))

    def sink_arrived(s, p, h):
        remote(sinkb.at[s, p, h], sinkb.at[s, p, h], sks.at[0, h], skr.at[s, p, h], partner).wait_recv()

    def chip_copy(h):
        block = sinkb.at[par, part, h]
        return remote(block, block, sks.at[0, h], skr.at[par, part, h], partner)

    def mate_copy(h):
        block = sinkb.at[par, part, h]
        return remote(block, block, sks.at[1, h], skr.at[par, part, h], member(2))

    def relay_copy(h):
        block = sinkb.at[par, y, h]
        return remote(block, block, sks.at[2, h], skr.at[par, y, h], partner)

    def kid_copy(i, kid, h):
        block = sinkb.at[par, part, h]
        return remote(block, block, skc.at[i, h], skr.at[par, part, h], at_plane(kid))

    def value_copy(i, h):
        block = sinkb.at[par, 0, h]
        return remote(block, block, crs.at[i, h], skr.at[par, 0, h], (16 + 2 * VALUE_KIDS[i] + par, g))

    def each_kid(body):
        for column, table in enumerate(KIDS):
            for at_z, kids in table.items():
                @pl.when(jnp.logical_and(y == column, z == at_z))
                def _():
                    for i, kid in enumerate(kids):
                        body(i, kid)

    has_mate = jnp.logical_or(y == 0, z > 0)

    def sink_send(h):
        each_kid(lambda i, kid: kid_copy(i, kid, h).start())
        gate((has_mate, mate_copy(h).start))
        chip_copy(h).start()

    def sink_pass(h):
        @pl.when(jnp.logical_not(owner))
        def _():
            sink_arrived(par, part, h)
            sink_send(h)

    def sink_relay(h):
        @pl.when(jnp.logical_not(owner))
        def _():
            sink_arrived(par, y, h)
            relay_copy(h).start()

    def inverse_copy(stretch):
        return remote(stat_inv, sinv.at[par], svs.at[stretch], svr.at[par], (stretch, g))

    def inverse_arrived(s):
        remote(sinv.at[s], sinv.at[s], svs.at[0], svr.at[s], partner).wait_recv()

    stat_inv = sinv.at[2]

    def each_other(body):
        def at(i, _):
            @pl.when(i != c)
            def _():
                body(i)

            return 0

        lax.fori_loop(0, STRETCHES, at, 0)

    def loop(count, step):
        lax.fori_loop(0, count, lambda h, _: (step(h), 0)[1], 0)

    def launch(h):
        @pl.when(owner)
        def _():
            for p in (0, 1):
                sinkb[par, p, h] = kv[h, p]
            for i in range(len(VALUE_KIDS)):
                value_copy(i, h).start()
            sink_send(h)
            relay_copy(h).start()

        gate((jnp.logical_or(h < AHEAD, jnp.logical_not(paced)), lambda: kv_send(h)))
        gate((jnp.logical_not(busy), lambda: qd_send(h)))

    def loop_from(low, high, step):
        lax.fori_loop(low, high, lambda h, _: (step(h), 0)[1], 0)

    reduce_start(0)
    loop_from(0, AHEAD, launch)

    for i, hbm in enumerate((query_gain_hbm, key_gain_hbm)):
        load_gain(i, hbm).wait()
    inverse = lax.rsqrt(reduce_finish(0) / D + EPS)
    sinv[2] = inverse

    @pl.when(owner)
    def _():
        sinv[par] = inverse
        each_other(lambda i: inverse_copy(i).start())

    def near_copy(i):
        shift = NEAR[i]
        return remote(sinv.at[2], ninv.at[i], nis.at[i], nir.at[i], dev(c + STRETCHES + shift))

    for i in range(len(NEAR)):
        near_copy(i).start()
    loop_from(AHEAD, HEADS, launch)
    inv[0] = to_full(inverse[0:1])
    inv[1] = to_full(inverse[1:2])

    def gain(i, h):
        return gains[i, pl.ds(pl.multiple_of(h * HDIM, HDIM), HDIM)].reshape(1, HDIM)

    def normed(block, full, i, h):
        return (block.astype(F32) * full * gain(i, h)).astype(BF16)

    def norms(h):
        queryn[h] = normed(qd[h, 1], inv[0], 0, h)
        keyn[h] = normed(kv[h, 1], inv[1], 1, h)

    loop(HEADS, norms)

    far = recent[0, 1]
    sink_id = sink[0, 0]
    far_two = jnp.logical_and(far == c - 2, c >= 2)
    far_three = jnp.logical_and(far == c - 3, c >= 3)
    two = jnp.where(far_two, 1.0, 0.0).astype(F32)
    sink_one = jnp.where(sink_id == 1, 1.0, 0.0).astype(F32)
    sink_zero = jnp.where(sink_id == 0, 1.0, 0.0).astype(F32)
    near_off = jnp.where(c >= 1, 0.0, FAR_AWAY).astype(F32)
    two_off = jnp.where(far_two, 0.0, FAR_AWAY).astype(F32)
    three_off = jnp.where(far_three, 0.0, FAR_AWAY).astype(F32)
    far_off = jnp.minimum(two_off, three_off)
    sink_off = jnp.where(sink_id >= 0, 0.0, FAR_AWAY).astype(F32)

    def blend(first, second, share):
        return first.astype(F32) * share + second.astype(F32) * (1.0 - share)

    def mix(first, second, share):
        return blend(first, second, share).astype(BF16)

    def key_side(keys, vals, queries, grads, log_row, delta_row):
        prob = jnp.exp2(dot_t(keys, queries) * SCALE2 - log_row)
        dprob = dot_t(vals, grads)
        dscore = (prob * (dprob - delta_row)).astype(BF16)
        return dot_n(dscore, queries), dot_n(prob.astype(BF16), grads)

    def stat_copy(shift, h):
        return remote(
            stat.at[h], statr.at[shift - 1, h], sts.at[shift - 1, h], strs.at[shift - 1, h],
            dev(c + STRETCHES - shift),
        )

    def partial_copy(i, h):
        s, p = (par + i % 2) % 2, 1 - (y + i // 2) % 2
        return remote(red.at[s, p, h], rr1.at[i - 1, h], rs1.at[i - 1, h], rr1s.at[i - 1, h], member(i))

    def query_side(h):
        gate((c >= 1, lambda: kv_arrived(0, h)), (c >= 3, lambda: kv_arrived(2, h)))
        for p in (0, 1):
            sink_arrived(1 - par, p, h)

        queries, grads = queryn[h], qd[h, 0]
        sink_raw = blend(sinkb[1, 1, h], sinkb[0, 1, h], sink_one) * gain(1, h)
        sink_keys = (sink_raw * inv[2]).astype(BF16)
        sink_vals = mix(sinkb[1, 0, h], sinkb[0, 0, h], sink_one)
        far_keys = normed(blend(kvr[1, h, 1], kvr[2, h, 1], two), inv[4], 1, h)
        blocks = (
            (keyn[h], kv[h, 0], 0.0),
            (normed(kvr[0, h, 1], inv[3], 1, h), kvr[0, h, 0], near_off),
            (far_keys, mix(kvr[1, h, 0], kvr[2, h, 0], two), far_off),
            (sink_keys, sink_vals, sink_off),
        )
        scores = [dot_t(queries, keys) * SCALE2 for keys, _, _ in blocks]
        top = None
        for score, block in zip(scores, blocks):
            here = jnp.max(score, axis=1, keepdims=True) - block[2]
            top = here if top is None else jnp.maximum(top, here)
        probs = [jnp.exp2(score - (top + block[2])) for score, block in zip(scores, blocks)]
        total = None
        for prob in probs:
            here = jnp.sum(prob, axis=1, keepdims=True)
            total = here if total is None else total + here
        share = 1.0 / total
        attended = jnp.zeros((TOKC, HDIM), F32)
        probs = [prob * share for prob in probs]
        for prob, block in zip(probs, blocks):
            attended = attended + dot_n(prob.astype(BF16), block[1])
        attended = attended.astype(BF16)
        att_out[:, pl.ds(pl.multiple_of(h * HDIM, HDIM), HDIM)] = attended
        delta = jnp.sum(grads.astype(F32) * attended.astype(F32), axis=1, keepdims=True)
        log_total = top + jnp.log2(total)
        rows = to_rows(
            (
                log_total, delta, log_total + near_off, log_total + two_off, log_total + three_off,
                log_total + sink_off,
            )
        )
        stat[h] = rows
        sink_dk, sink_dv = key_side(sink_keys, sink_vals, queries, grads, rows[5:6], rows[1:2])
        tsum[...] = tsum[...] + sink_dk * sink_raw
        for s, mine in ((0, sink_zero), (1, sink_one)):
            red[s, 1, h] = (sink_dk * mine).astype(BF16)
            red[s, 0, h] = (sink_dv * mine).astype(BF16)
        for i in (2, 3, 1):
            partial_copy(i, h).start()
        for shift in (1, 2, 3):
            stat_copy(shift, h).start()

        query_delta = jnp.zeros((TOKC, HDIM), F32)
        for prob, block in zip(probs, blocks):
            dscore = (prob * (dot_t(grads, block[1]) - delta)).astype(BF16)
            query_delta = query_delta + dot_n(dscore, block[0])
        dq[h] = query_delta * SCALE

    def owner_side(h):
        keys, vals = keyn[h], kv[h, 0]
        key_sum, value_sum = key_side(keys, vals, queryn[h], qd[h, 0], stat[h, 0:1], stat[h, 1:2])
        for slot in range(3):
            if slot != 1:
                gate((c <= 30 - slot, lambda: qd_arrived(slot, h)))
            stat_copy(slot + 1, h).wait_recv()
            more_keys, more_values = key_side(
                keys, vals, normed(qdr[slot, h, 1], inv[5 + slot], 0, h), qdr[slot, h, 0],
                statr[slot, h, slot + 2:slot + 3], statr[slot, h, 1:2],
            )
            key_sum, value_sum = key_sum + more_keys, value_sum + more_values
        dk[h] = key_sum
        dv[h] = value_sum

    def up_copy(slot, parent, h):
        return remote(up.at[h], rr2.at[slot, h], rs2.at[h], rr2s.at[slot, h], at_plane(parent))

    def each_parent(body):
        for parent, below in SUMS.items():
            for slot, kid in enumerate(below):
                @pl.when(z == kid)
                def _():
                    body(slot, parent)

    def up_send(h):
        up[h] = acc[h].astype(BF16)
        each_parent(lambda slot, parent: up_copy(slot, parent, h).start())

    def plane_sum(h):
        total = red[par, part, h].astype(F32)
        for slot in range(3):
            remote(rr1.at[slot, h], rr1.at[slot, h], rs1.at[0, h], rr1s.at[slot, h], partner).wait_recv()
            total = total + rr1[slot, h].astype(F32)
        acc[h] = total

        @pl.when(is_leaf)
        def _():
            up_send(h)

    def below_sum(h, count):
        total = acc[h]
        for slot in range(count):
            remote(rr2.at[slot, h], rr2.at[slot, h], rs2.at[h], rr2s.at[slot, h], partner).wait_recv()
            total = total + rr2[slot, h].astype(F32)
        acc[h] = total

    def value_back(h):
        return remote(up.at[h], vin.at[h], vis.at[h], vir.at[h], (par, g))

    is_leaf = z < 0
    for at_z in range(1, 8):
        if at_z not in SUMS:
            is_leaf = jnp.logical_or(is_leaf, z == at_z)

    def when_in(at, low, body):
        @pl.when(jnp.logical_and(at >= low, at < low + HEADS))
        def _():
            body(at - low)

    def middle(h):
        for at_z in SUMS:
            if at_z:
                @pl.when(z == at_z)
                def _():
                    below_sum(h, len(SUMS[at_z]))
                    up_send(h)

    def finish(h):
        below_sum(h, len(SUMS[0]))

        @pl.when(y == 0)
        def _():
            dk[h] = dk[h] + acc[h]

        @pl.when(y == 1)
        def _():
            up[h] = acc[h].astype(BF16)
            value_back(h).start()

    def prepare():
        @pl.when(c != 0)
        def _():
            inverse_arrived(0)

        @pl.when(c != 1)
        def _():
            inverse_arrived(1)

        for i in range(len(NEAR)):
            near_copy(i).wait_recv()
        inv[2] = to_full(sinv[1, 1:2] * sink_one + sinv[0, 1:2] * (1.0 - sink_one))
        inv[3] = to_full(ninv[0, 1:2])
        inv[4] = to_full(ninv[1, 1:2] * two + ninv[2, 1:2] * (1.0 - two))
        for slot in range(3):
            inv[5 + slot] = to_full(ninv[3 + slot, 0:1])

    tsum[...] = jnp.zeros((TOKC, HDIM), F32)

    def tile_copy(root):
        return remote(tout, tin.at[c], tis.at[root], tir.at[c], (root, g))

    def tile_send():
        sink_inner = jnp.sum(tsum[...], axis=1, keepdims=True) * SCALE
        tout[...] = to_rows((sink_inner * sink_zero, sink_inner * sink_one))
        for root in (0, 1):
            @pl.when(c != root)
            def _():
                tile_copy(root).start()

    def step(at):
        when_in(at, 0, kv_forward)
        when_in(at, lag_pass, sink_pass)
        gate((jnp.logical_and(paced, at < HEADS - AHEAD), lambda: kv_send(at + AHEAD)))
        when_in(at, lag_relay, sink_relay)
        when_in(at, lag_pass, lambda h: gate((busy, lambda: qd_send(h))))

        @pl.when(at == lag_query)
        def _():
            prepare()

        when_in(at, lag_query, query_side)
        gate((at == lag_query + HEADS - 1, tile_send))
        when_in(at, lag_query + 1, plane_sum)
        when_in(at, 9, middle)
        when_in(at, 7, qd_forward)
        when_in(at, lag_owner, owner_side)

    loop(HEADS + 11, step)

    def inner(h, sums):
        return (
            sums[0] + dq[h] * (gain(0, h) * qd[h, 1].astype(F32)),
            sums[1] + dk[h] * (gain(1, h) * SCALE * kv[h, 1].astype(F32)),
        )

    sums = lax.fori_loop(0, HEADS, inner, (zeros, zeros))
    tile[1] = to_rows([jnp.sum(part_sum, axis=1, keepdims=True) for part_sum in sums])

    @pl.when(owner)
    def _():
        tin[c] = tout[...]

        def gather(i):
            remote(tin.at[i], tin.at[i], tis.at[0], tir.at[i], partner).wait_recv()
            tin[c] = tin[c] + tin[i]

        each_other(gather)
        sums = tin[c]
        mine = jnp.where(odd, 1.0, 0.0).astype(F32)
        row = sums[0:1] * (1.0 - mine) + sums[1:2] * mine
        level = lax.broadcasted_iota(jnp.int32, (8, TOKC), 0)
        tile[1] = tile[1] + jnp.where(level == 1, row, 0.0)

    reduce_start(1)
    gate((jnp.logical_and(z == 0, y == 1), lambda: loop(HEADS, finish)))
    total = reduce_finish(1)
    query_inner = to_full(total[0:1]) * inv[0] * inv[0] * inv[0] / D
    inv[2] = to_full(total[1:2]) * inv[1] * inv[1] * inv[1] / D
    for h in range(HEADS):
        at = pl.ds(h * HDIM, HDIM)
        dq_out[:, at] = (dq[h] * gain(0, h) * inv[0] - qd[h, 1].astype(F32) * query_inner).astype(BF16)

    gate((owner, lambda: loop(HEADS, finish)))

    for h in range(HEADS):
        at = pl.ds(h * HDIM, HDIM)
        dk_out[:, at] = (dk[h] * SCALE * gain(1, h) * inv[1] - kv[h, 1].astype(F32) * inv[2]).astype(BF16)

    @pl.when(owner)
    def _():
        for h in range(HEADS):
            value_back(h).wait_recv()
            dv[h] = dv[h] + vin[h].astype(F32)

    for h in range(HEADS):
        dv_out[:, pl.ds(h * HDIM, HDIM)] = dv[h].astype(BF16)

    def drain(h):
        gate(
            (c <= 29, kv_own(h).wait_send), (jnp.logical_or(even, kv_on), kv_beside(h).wait_send),
            (kv_has, kv_across(h).wait_send), (c >= 2, qd_own(h).wait_send),
            (jnp.logical_or(odd, qd_on), qd_beside(h).wait_send), (qd_has, qd_across(h).wait_send),
            (has_mate, mate_copy(h).wait_send),
        )
        each_kid(lambda i, kid: kid_copy(i, kid, h).wait_send())
        chip_copy(h).wait_send()
        relay_copy(h).wait_send()
        for i in (1, 2, 3):
            partial_copy(i, h).wait_send()
            stat_copy(i, h).wait_send()
        each_parent(lambda slot, parent: up_copy(slot, parent, h).wait_send())

        @pl.when(owner)
        def _():
            for i in range(len(VALUE_KIDS)):
                value_copy(i, h).wait_send()

        @pl.when(jnp.logical_and(z == 0, y == 1))
        def _():
            value_back(h).wait_send()

    loop(HEADS, drain)

    @pl.when(owner)
    def _():
        each_other(lambda i: inverse_copy(i).wait_send())

    for root in (0, 1):
        @pl.when(c != root)
        def _():
            tile_copy(root).wait_send()

    for i in range(len(NEAR)):
        near_copy(i).wait_send()
    for phase in (0, 1):
        for shift in range(1, HEAD_DEVICES):
            reduce_copy(phase, shift).wait_send()


def hand_on(*refs):
    held, sem = refs[8:]
    reads = [pltpu.make_async_copy(refs[i], held.at[i], sem.at[0, i]) for i in range(4)]
    writes = [pltpu.make_async_copy(held.at[i], refs[4 + i], sem.at[1, i]) for i in range(4)]
    for read in reads:
        read.start()
    for read, write in zip(reads, writes):
        read.wait()
        write.start()
    for write in writes:
        write.wait()


def per_device(query_raw, key_raw, values, query_gain, key_gain, recent_ids, sink_ids, out_grad):
    rows, width = query_raw.shape
    block = (HEADS, TOKC, HDIM)
    pair = (HEADS, 2, TOKC, HDIM)
    dma = pltpu.SemaphoreType.DMA
    any_spec = pl.BlockSpec(memory_space=pltpu.HBM)
    vmem = pl.BlockSpec(memory_space=pltpu.VMEM)
    smem = pl.BlockSpec(memory_space=pltpu.SMEM)
    outputs = pl.pallas_call(
        kernel,
        out_shape=[jax.ShapeDtypeStruct((rows, width), BF16)] * 4,
        in_specs=[any_spec] * 6 + [smem] * 2,
        out_specs=[vmem] * 4,
        scratch_shapes=[
            pltpu.VMEM(pair, BF16),
            pltpu.VMEM(pair, BF16),
            pltpu.VMEM(block, BF16),
            pltpu.VMEM(block, BF16),
            pltpu.VMEM((3,) + pair, BF16),
            pltpu.VMEM((3,) + pair, BF16),
            pltpu.VMEM((2, 2) + block, BF16),
            pltpu.VMEM((2, 2) + block, BF16),
            pltpu.VMEM((3,) + block, BF16),
            pltpu.VMEM((3,) + block, BF16),
            pltpu.VMEM(block, F32),
            pltpu.VMEM(block, BF16),
            pltpu.VMEM(block, BF16),
            pltpu.VMEM(block, F32),
            pltpu.VMEM(block, F32),
            pltpu.VMEM(block, F32),
            pltpu.VMEM((HEADS, 8, TOKC), F32),
            pltpu.VMEM((3, HEADS, 8, TOKC), F32),
            pltpu.VMEM((2, 8, TOKC), F32),
            pltpu.VMEM((2, HEAD_DEVICES - 1, 8, TOKC), F32),
            pltpu.VMEM((8, TOKC, HDIM), F32),
            pltpu.VMEM((2, width), F32),
            pltpu.VMEM((3, 8, TOKC), F32),
            pltpu.VMEM((len(NEAR), 8, TOKC), F32),
            pltpu.VMEM((TOKC, HDIM), F32),
            pltpu.VMEM((8, TOKC), F32),
            pltpu.VMEM((STRETCHES, 8, TOKC), F32),
            dma((4, HEADS)),
            dma((2,)),
            dma((3, HEADS)),
            dma((3, HEADS)),
            dma((3, HEADS)),
            dma((3, HEADS)),
            dma((3, HEADS)),
            dma((3, HEADS)),
            dma((2, 2, HEADS)),
            dma((3, HEADS)),
            dma((3, HEADS)),
            dma((2, HEAD_DEVICES - 1)),
            dma((2, HEAD_DEVICES - 1)),
            dma((3, HEADS)),
            dma((3, HEADS)),
            dma((HEADS,)),
            dma((3, HEADS)),
            dma((HEADS,)),
            dma((HEADS,)),
            dma((len(VALUE_KIDS), HEADS)),
            dma((STRETCHES,)),
            dma((2,)),
            dma((2,)),
            dma((STRETCHES,)),
            dma((len(NEAR),)),
            dma((len(NEAR),)),
        ],
        compiler_params=pltpu.CompilerParams(
            collective_id=0, has_side_effects=True, vmem_limit_bytes=60 * 2**20
        ),
        cost_estimate=pl.CostEstimate(flops=3 * 10**9, bytes_accessed=6 * 10**6, transcendentals=3 * 10**6),
        name="stretch_attention",
    )(
        query_raw, key_raw, values, out_grad, query_gain, key_gain, recent_ids, sink_ids,
    )
    return pl.pallas_call(
        hand_on,
        out_shape=[jax.ShapeDtypeStruct((rows, width), BF16)] * 4,
        in_specs=[any_spec] * 4,
        out_specs=[any_spec] * 4,
        scratch_shapes=[pltpu.VMEM((4, rows, width), BF16), dma((2, 4))],
        name="hand_on",
    )(*outputs)


def solution(mesh):
    split = P("stretch", "head")
    return jax.shard_map(
        per_device,
        mesh=mesh,
        in_specs=(split, split, split, P("head"), P("head"), P("stretch", None), P("stretch", None), split),
        out_specs=(split,) * 4,
        check_vma=False,
    )
```

```python
import jax
import jax.numpy as jnp
from jax import lax
from jax.experimental import pallas as pl
from jax.experimental.pallas import tpu as pltpu
from jax.sharding import PartitionSpec as P

D = 5120
HDIM = 128
TOKC = 256
HEADS = 5
STRETCHES = 32
HEAD_DEVICES = 8
EPS = 1e-06
SCALE = HDIM ** (-0.5)
SCALE2 = SCALE * 1.4426950408889634
FAR_AWAY = 1e30
MESH = pl.DeviceIdType.MESH
NEAR = (1, 2, 3, -1, -2, -3)
KIDS = ({0: (1, 7), 1: (2,), 7: (6, 5), 5: (4, 3)}, {1: (2,), 7: (6, 5, 0), 5: (4, 3)})
VALUE_KIDS = (1, 7)
AHEAD = 4
SUMS = {0: (1, 7, 5), 1: (2,), 7: (6,), 5: (4, 3)}
F32 = jnp.float32
BF16 = jnp.bfloat16


def dot_t(a, b):
    return lax.dot_general(a, b, (((1,), (1,)), ((), ())), preferred_element_type=F32)


def dot_n(a, b):
    return lax.dot_general(a, b, (((1,), (0,)), ((), ())), preferred_element_type=F32)


def to_rows(columns):
    lane = lax.broadcasted_iota(jnp.int32, (TOKC, HDIM), 1)
    spread = jnp.zeros((TOKC, HDIM), F32)
    for i, column in enumerate(columns):
        spread = jnp.where(lane == i, column, spread)
    return spread.T[:8]


def to_full(row):
    return jnp.broadcast_to(row, (HDIM, TOKC)).T


def remote(src, dst, send, recv, device):
    return pltpu.make_async_remote_copy(
        src_ref=src, dst_ref=dst, send_sem=send, recv_sem=recv, device_id=device, device_id_type=MESH
    )


def kernel(
    query_hbm, key_hbm, values_hbm, grad_hbm, query_gain_hbm, key_gain_hbm, recent, sink,
    att_out, dq_out, dk_out, dv_out,
    kv, qd, keyn, queryn, kvr, qdr, sinkb, red, rr1, rr2, acc, up, vin, dq, dk, dv, stat, statr, tile, tiler, inv, gains, sinv, ninv, tsum, tout, tin,
    load_sem, gain_sem, kvs, kvrs, qds, qdrs, sks, skc, skr, sts, strs, ars, arr, rs1, rr1s, rs2, rr2s, vis, vir, crs, svs, svr, tis, tir, nis, nir,
):
    c = lax.axis_index("stretch")
    g = lax.axis_index("head")
    par = c % 2
    z = (c // 2) % 8
    y = c // 16
    part = 1 - y
    even = par == 0
    odd = par == 1
    owner = c < 2
    partner = (c + 1 - 2 * par, g)

    def dev(stretch):
        return (stretch % STRETCHES, g)

    def member(i):
        return (((y + i // 2) % 2) * 16 + 2 * z + (par + i % 2) % 2, g)

    def at_plane(other):
        return (y * 16 + 2 * other + par, g)

    loads = ((values_hbm, kv, 0), (key_hbm, kv, 1), (query_hbm, qd, 1), (grad_hbm, qd, 0))
    level = jnp.where((z == 1) | (z == 7), 1, jnp.where((z == 4) | (z == 3), 3, 2))
    level = jnp.where(owner, 0, level)
    lag_pass = jnp.where(owner, 0, 2 * level - 2)
    lag_relay = 2 * level
    lag_query = jnp.where(owner, 2, 2 * level + 1)
    paced = z == 1
    busy = z >= 4
    lag_owner = jnp.where(level == 3, 11, 9)

    def load(i, h):
        hbm, dst, p = loads[i]
        return pltpu.make_async_copy(hbm.at[:, pl.ds(h * HDIM, HDIM)], dst.at[h, p], load_sem.at[i, h])

    def load_gain(i, hbm):
        return pltpu.make_async_copy(hbm, gains.at[i], gain_sem.at[i])

    for i in (1, 2, 0, 3):
        for h in range(HEADS):
            load(i, h).start()
    load_gain(0, query_gain_hbm).start()
    load_gain(1, key_gain_hbm).start()

    for missing, buffer, slot in (
        (c == 0, kvr, 0), (c < 2, kvr, 1), (c < 3, kvr, 2), (c > 30, qdr, 0), (c > 29, qdr, 1), (c > 28, qdr, 2),
    ):
        @pl.when(missing)
        def _():
            buffer[slot] = jnp.zeros((HEADS, 2, TOKC, HDIM), BF16)

    barrier = pltpu.get_barrier_semaphore()

    def greet(device):
        pl.semaphore_signal(barrier, inc=1, device_id=device, device_id_type=MESH)

    for shift in (1, 2, 3):
        greet(dev(c + shift))
        greet(dev(c - shift + STRETCHES))
    for i in (1, 2, 3):
        greet(member(i))
    for shift in range(1, HEAD_DEVICES):
        greet((c, (g + shift) % HEAD_DEVICES))

    def greet_all(i, _):
        @pl.when(i != c)
        def _():
            greet((i, g))

        return 0

    @pl.when(owner)
    def _():
        lax.fori_loop(0, STRETCHES, greet_all, 0)

    for root in (0, 1):
        @pl.when(c != root)
        def _():
            greet((root, g))

    degree = jnp.where(owner, STRETCHES, 2)
    for at_z in range(8):
        friends = sorted(set(KIDS[0].get(at_z, ()) + SUMS.get(at_z, ()) + tuple(
            top for table in (KIDS[0], SUMS) for top, below in table.items() if at_z in below)))
        degree = degree + jnp.where(z == at_z, len(friends), 0)

        @pl.when(z == at_z)
        def _():
            for friend in friends:
                greet(at_plane(friend))

    for h in range(HEADS):
        for i in (1, 2, 0, 3):
            load(i, h).wait()

    def square(block):
        block = block.astype(F32)
        return block * block

    def squares(h, sums):
        return sums[0] + square(qd[h, 1]), sums[1] + square(kv[h, 1])

    zeros = jnp.zeros((TOKC, HDIM), F32)
    sums = lax.fori_loop(0, HEADS, squares, (zeros, zeros))
    tile[0] = to_rows([jnp.sum(part_sum, axis=1, keepdims=True) for part_sum in sums])
    pl.semaphore_wait(barrier, 16 + degree)

    def reduce_copy(phase, shift):
        return remote(
            tile.at[phase], tiler.at[phase, shift - 1], ars.at[phase, shift - 1], arr.at[phase, shift - 1],
            (c, (g + shift) % HEAD_DEVICES),
        )

    def reduce_start(phase):
        for shift in range(1, HEAD_DEVICES):
            reduce_copy(phase, shift).start()

    def reduce_finish(phase):
        total = tile[phase]
        for shift in range(1, HEAD_DEVICES):
            reduce_copy(phase, shift).wait_recv()
            total = total + tiler[phase, shift - 1]
        return total

    def kv_own(h):
        return remote(kv.at[h], kvr.at[1, h], kvs.at[0, h], kvrs.at[1, h], dev(c + 2))

    def kv_beside(h):
        return remote(kv.at[h], kvr.at[0, h], kvs.at[1, h], kvrs.at[0, h], dev(c + 1))

    def kv_onward(h):
        return remote(kvr.at[1, h], kvr.at[2, h], kvs.at[1, h], kvrs.at[2, h], dev(c + 1))

    def kv_across(h):
        slot = 2 - 2 * par
        return remote(kvr.at[1, h], kvr.at[slot, h], kvs.at[2, h], kvrs.at[slot, h], partner)

    def qd_own(h):
        return remote(qd.at[h], qdr.at[1, h], qds.at[0, h], qdrs.at[1, h], dev(c + STRETCHES - 2))

    def qd_beside(h):
        return remote(qd.at[h], qdr.at[0, h], qds.at[1, h], qdrs.at[0, h], dev(c + STRETCHES - 1))

    def qd_onward(h):
        return remote(qdr.at[1, h], qdr.at[2, h], qds.at[1, h], qdrs.at[2, h], dev(c + STRETCHES - 1))

    def qd_across(h):
        slot = 2 * par
        return remote(qdr.at[1, h], qdr.at[slot, h], qds.at[2, h], qdrs.at[slot, h], partner)

    def kv_arrived(slot, h):
        remote(kvr.at[slot, h], kvr.at[slot, h], kvs.at[0, h], kvrs.at[slot, h], partner).wait_recv()

    def qd_arrived(slot, h):
        remote(qdr.at[slot, h], qdr.at[slot, h], qds.at[0, h], qdrs.at[slot, h], partner).wait_recv()

    def gate(*steps):
        for condition, action in steps:
            pl.when(condition)(lambda act=action: (act(), None)[1])

    kv_has, qd_has = c >= 2, c <= 29
    kv_on = jnp.logical_and(odd, jnp.logical_and(c >= 3, c <= 29))
    qd_on = jnp.logical_and(even, jnp.logical_and(c >= 2, c <= 28))

    def kv_send(h):
        gate((c <= 29, kv_own(h).start), (even, kv_beside(h).start))

    def kv_forward(h):
        gate((kv_has, lambda: kv_arrived(1, h)), (kv_on, kv_onward(h).start), (kv_has, kv_across(h).start))

    def qd_send(h):
        gate((c >= 2, qd_own(h).start), (odd, qd_beside(h).start))

    def qd_forward(h):
        gate((qd_has, lambda: qd_arrived(1, h)), (qd_on, qd_onward(h).start), (qd_has, qd_across(h).start))

    def sink_arrived(s, p, h):
        remote(sinkb.at[s, p, h], sinkb.at[s, p, h], sks.at[0, h], skr.at[s, p, h], partner).wait_recv()

    def chip_copy(h):
        block = sinkb.at[par, part, h]
        return remote(block, block, sks.at[0, h], skr.at[par, part, h], partner)

    def mate_copy(h):
        block = sinkb.at[par, part, h]
        return remote(block, block, sks.at[1, h], skr.at[par, part, h], member(2))

    def relay_copy(h):
        block = sinkb.at[par, y, h]
        return remote(block, block, sks.at[2, h], skr.at[par, y, h], partner)

    def kid_copy(i, kid, h):
        block = sinkb.at[par, part, h]
        return remote(block, block, skc.at[i, h], skr.at[par, part, h], at_plane(kid))

    def value_copy(i, h):
        block = sinkb.at[par, 0, h]
        return remote(block, block, crs.at[i, h], skr.at[par, 0, h], (16 + 2 * VALUE_KIDS[i] + par, g))

    def each_kid(body):
        for column, table in enumerate(KIDS):
            for at_z, kids in table.items():
                @pl.when(jnp.logical_and(y == column, z == at_z))
                def _():
                    for i, kid in enumerate(kids):
                        body(i, kid)

    has_mate = jnp.logical_or(y == 0, z > 0)

    def sink_send(h):
        each_kid(lambda i, kid: kid_copy(i, kid, h).start())
        gate((has_mate, mate_copy(h).start))
        chip_copy(h).start()

    def sink_pass(h):
        @pl.when(jnp.logical_not(owner))
        def _():
            sink_arrived(par, part, h)
            sink_send(h)

    def sink_relay(h):
        @pl.when(jnp.logical_not(owner))
        def _():
            sink_arrived(par, y, h)
            relay_copy(h).start()

    def inverse_copy(stretch):
        return remote(stat_inv, sinv.at[par], svs.at[stretch], svr.at[par], (stretch, g))

    def inverse_arrived(s):
        remote(sinv.at[s], sinv.at[s], svs.at[0], svr.at[s], partner).wait_recv()

    stat_inv = sinv.at[2]

    def each_other(body):
        def at(i, _):
            @pl.when(i != c)
            def _():
                body(i)

            return 0

        lax.fori_loop(0, STRETCHES, at, 0)

    def loop(count, step):
        lax.fori_loop(0, count, lambda h, _: (step(h), 0)[1], 0)

    def launch(h):
        @pl.when(owner)
        def _():
            for p in (0, 1):
                sinkb[par, p, h] = kv[h, p]
            for i in range(len(VALUE_KIDS)):
                value_copy(i, h).start()
            sink_send(h)
            relay_copy(h).start()

        gate((jnp.logical_or(h < AHEAD, jnp.logical_not(paced)), lambda: kv_send(h)))
        gate((jnp.logical_not(busy), lambda: qd_send(h)))

    def loop_from(low, high, step):
        lax.fori_loop(low, high, lambda h, _: (step(h), 0)[1], 0)

    reduce_start(0)
    loop_from(0, AHEAD, launch)

    for i, hbm in enumerate((query_gain_hbm, key_gain_hbm)):
        load_gain(i, hbm).wait()
    inverse = lax.rsqrt(reduce_finish(0) / D + EPS)
    sinv[2] = inverse

    @pl.when(owner)
    def _():
        sinv[par] = inverse
        each_other(lambda i: inverse_copy(i).start())

    def near_copy(i):
        shift = NEAR[i]
        return remote(sinv.at[2], ninv.at[i], nis.at[i], nir.at[i], dev(c + STRETCHES + shift))

    for i in range(len(NEAR)):
        near_copy(i).start()
    loop_from(AHEAD, HEADS, launch)
    inv[0] = to_full(inverse[0:1])
    inv[1] = to_full(inverse[1:2])

    def gain(i, h):
        return gains[i, pl.ds(pl.multiple_of(h * HDIM, HDIM), HDIM)].reshape(1, HDIM)

    def normed(block, full, i, h):
        return (block.astype(F32) * full * gain(i, h)).astype(BF16)

    def norms(h):
        queryn[h] = normed(qd[h, 1], inv[0], 0, h)
        keyn[h] = normed(kv[h, 1], inv[1], 1, h)

    loop(HEADS, norms)

    far = recent[0, 1]
    sink_id = sink[0, 0]
    far_two = jnp.logical_and(far == c - 2, c >= 2)
    far_three = jnp.logical_and(far == c - 3, c >= 3)
    two = jnp.where(far_two, 1.0, 0.0).astype(F32)
    sink_one = jnp.where(sink_id == 1, 1.0, 0.0).astype(F32)
    sink_zero = jnp.where(sink_id == 0, 1.0, 0.0).astype(F32)
    near_off = jnp.where(c >= 1, 0.0, FAR_AWAY).astype(F32)
    two_off = jnp.where(far_two, 0.0, FAR_AWAY).astype(F32)
    three_off = jnp.where(far_three, 0.0, FAR_AWAY).astype(F32)
    far_off = jnp.minimum(two_off, three_off)
    sink_off = jnp.where(sink_id >= 0, 0.0, FAR_AWAY).astype(F32)

    def blend(first, second, share):
        return first.astype(F32) * share + second.astype(F32) * (1.0 - share)

    def mix(first, second, share):
        return blend(first, second, share).astype(BF16)

    def key_side(keys, vals, queries, grads, log_row, delta_row):
        prob = jnp.exp2(dot_t(keys, queries) * SCALE2 - log_row)
        dprob = dot_t(vals, grads)
        dscore = (prob * (dprob - delta_row)).astype(BF16)
        return dot_n(dscore, queries), dot_n(prob.astype(BF16), grads)

    def stat_copy(shift, h):
        return remote(
            stat.at[h], statr.at[shift - 1, h], sts.at[shift - 1, h], strs.at[shift - 1, h],
            dev(c + STRETCHES - shift),
        )

    def partial_copy(i, h):
        s, p = (par + i % 2) % 2, 1 - (y + i // 2) % 2
        return remote(red.at[s, p, h], rr1.at[i - 1, h], rs1.at[i - 1, h], rr1s.at[i - 1, h], member(i))

    def query_side(h):
        gate((c >= 1, lambda: kv_arrived(0, h)), (c >= 3, lambda: kv_arrived(2, h)))
        for p in (0, 1):
            sink_arrived(1 - par, p, h)

        queries, grads = queryn[h], qd[h, 0]
        sink_raw = blend(sinkb[1, 1, h], sinkb[0, 1, h], sink_one) * gain(1, h)
        sink_keys = (sink_raw * inv[2]).astype(BF16)
        sink_vals = mix(sinkb[1, 0, h], sinkb[0, 0, h], sink_one)
        far_keys = normed(blend(kvr[1, h, 1], kvr[2, h, 1], two), inv[4], 1, h)
        blocks = (
            (keyn[h], kv[h, 0], 0.0),
            (normed(kvr[0, h, 1], inv[3], 1, h), kvr[0, h, 0], near_off),
            (far_keys, mix(kvr[1, h, 0], kvr[2, h, 0], two), far_off),
            (sink_keys, sink_vals, sink_off),
        )
        scores = [dot_t(queries, keys) * SCALE2 for keys, _, _ in blocks]
        top = None
        for score, block in zip(scores, blocks):
            here = jnp.max(score, axis=1, keepdims=True) - block[2]
            top = here if top is None else jnp.maximum(top, here)
        probs = [jnp.exp2(score - (top + block[2])) for score, block in zip(scores, blocks)]
        total = None
        for prob in probs:
            here = jnp.sum(prob, axis=1, keepdims=True)
            total = here if total is None else total + here
        share = 1.0 / total
        attended = jnp.zeros((TOKC, HDIM), F32)
        probs = [prob * share for prob in probs]
        for prob, block in zip(probs, blocks):
            attended = attended + dot_n(prob.astype(BF16), block[1])
        attended = attended.astype(BF16)
        att_out[:, pl.ds(pl.multiple_of(h * HDIM, HDIM), HDIM)] = attended
        delta = jnp.sum(grads.astype(F32) * attended.astype(F32), axis=1, keepdims=True)
        log_total = top + jnp.log2(total)
        rows = to_rows(
            (
                log_total, delta, log_total + near_off, log_total + two_off, log_total + three_off,
                log_total + sink_off,
            )
        )
        stat[h] = rows
        sink_dk, sink_dv = key_side(sink_keys, sink_vals, queries, grads, rows[5:6], rows[1:2])
        tsum[...] = tsum[...] + sink_dk * sink_raw
        for s, mine in ((0, sink_zero), (1, sink_one)):
            red[s, 1, h] = (sink_dk * mine).astype(BF16)
            red[s, 0, h] = (sink_dv * mine).astype(BF16)
        for i in (2, 3, 1):
            partial_copy(i, h).start()
        for shift in (1, 2, 3):
            stat_copy(shift, h).start()

        query_delta = jnp.zeros((TOKC, HDIM), F32)
        for prob, block in zip(probs, blocks):
            dscore = (prob * (dot_t(grads, block[1]) - delta)).astype(BF16)
            query_delta = query_delta + dot_n(dscore, block[0])
        dq[h] = query_delta * SCALE

    def owner_side(h):
        keys, vals = keyn[h], kv[h, 0]
        key_sum, value_sum = key_side(keys, vals, queryn[h], qd[h, 0], stat[h, 0:1], stat[h, 1:2])
        for slot in range(3):
            if slot != 1:
                gate((c <= 30 - slot, lambda: qd_arrived(slot, h)))
            stat_copy(slot + 1, h).wait_recv()
            more_keys, more_values = key_side(
                keys, vals, normed(qdr[slot, h, 1], inv[5 + slot], 0, h), qdr[slot, h, 0],
                statr[slot, h, slot + 2:slot + 3], statr[slot, h, 1:2],
            )
            key_sum, value_sum = key_sum + more_keys, value_sum + more_values
        dk[h] = key_sum
        dv[h] = value_sum

    def up_copy(slot, parent, h):
        return remote(up.at[h], rr2.at[slot, h], rs2.at[h], rr2s.at[slot, h], at_plane(parent))

    def each_parent(body):
        for parent, below in SUMS.items():
            for slot, kid in enumerate(below):
                @pl.when(z == kid)
                def _():
                    body(slot, parent)

    def up_send(h):
        up[h] = acc[h].astype(BF16)
        each_parent(lambda slot, parent: up_copy(slot, parent, h).start())

    def plane_sum(h):
        total = red[par, part, h].astype(F32)
        for slot in range(3):
            remote(rr1.at[slot, h], rr1.at[slot, h], rs1.at[0, h], rr1s.at[slot, h], partner).wait_recv()
            total = total + rr1[slot, h].astype(F32)
        acc[h] = total

        @pl.when(is_leaf)
        def _():
            up_send(h)

    def below_sum(h, count):
        total = acc[h]
        for slot in range(count):
            remote(rr2.at[slot, h], rr2.at[slot, h], rs2.at[h], rr2s.at[slot, h], partner).wait_recv()
            total = total + rr2[slot, h].astype(F32)
        acc[h] = total

    def value_back(h):
        return remote(up.at[h], vin.at[h], vis.at[h], vir.at[h], (par, g))

    is_leaf = z < 0
    for at_z in range(1, 8):
        if at_z not in SUMS:
            is_leaf = jnp.logical_or(is_leaf, z == at_z)

    def when_in(at, low, body):
        @pl.when(jnp.logical_and(at >= low, at < low + HEADS))
        def _():
            body(at - low)

    def middle(h):
        for at_z in SUMS:
            if at_z:
                @pl.when(z == at_z)
                def _():
                    below_sum(h, len(SUMS[at_z]))
                    up_send(h)

    def finish(h):
        below_sum(h, len(SUMS[0]))

        @pl.when(y == 0)
        def _():
            dk[h] = dk[h] + acc[h]

        @pl.when(y == 1)
        def _():
            up[h] = acc[h].astype(BF16)
            value_back(h).start()

    def prepare():
        @pl.when(c != 0)
        def _():
            inverse_arrived(0)

        @pl.when(c != 1)
        def _():
            inverse_arrived(1)

        for i in range(len(NEAR)):
            near_copy(i).wait_recv()
        inv[2] = to_full(sinv[1, 1:2] * sink_one + sinv[0, 1:2] * (1.0 - sink_one))
        inv[3] = to_full(ninv[0, 1:2])
        inv[4] = to_full(ninv[1, 1:2] * two + ninv[2, 1:2] * (1.0 - two))
        for slot in range(3):
            inv[5 + slot] = to_full(ninv[3 + slot, 0:1])

    tsum[...] = jnp.zeros((TOKC, HDIM), F32)

    def tile_copy(root):
        return remote(tout, tin.at[c], tis.at[root], tir.at[c], (root, g))

    def tile_send():
        sink_inner = jnp.sum(tsum[...], axis=1, keepdims=True) * SCALE
        tout[...] = to_rows((sink_inner * sink_zero, sink_inner * sink_one))
        for root in (0, 1):
            @pl.when(c != root)
            def _():
                tile_copy(root).start()

    def step(at):
        when_in(at, 0, kv_forward)
        when_in(at, lag_pass, sink_pass)
        gate((jnp.logical_and(paced, at < HEADS - AHEAD), lambda: kv_send(at + AHEAD)))
        when_in(at, lag_relay, sink_relay)
        when_in(at, 1, lambda h: gate((busy, lambda: qd_send(h))))

        @pl.when(at == lag_query)
        def _():
            prepare()

        when_in(at, lag_query, query_side)
        gate((at == lag_query + HEADS - 1, tile_send))
        when_in(at, lag_query + 1, plane_sum)
        when_in(at, 9, middle)
        when_in(at, 7, qd_forward)
        when_in(at, lag_owner, owner_side)

    loop(HEADS + 11, step)

    def inner(h, sums):
        return (
            sums[0] + dq[h] * (gain(0, h) * qd[h, 1].astype(F32)),
            sums[1] + dk[h] * (gain(1, h) * SCALE * kv[h, 1].astype(F32)),
        )

    sums = lax.fori_loop(0, HEADS, inner, (zeros, zeros))
    tile[1] = to_rows([jnp.sum(part_sum, axis=1, keepdims=True) for part_sum in sums])

    @pl.when(owner)
    def _():
        tin[c] = tout[...]

        def gather(i):
            remote(tin.at[i], tin.at[i], tis.at[0], tir.at[i], partner).wait_recv()
            tin[c] = tin[c] + tin[i]

        each_other(gather)
        sums = tin[c]
        mine = jnp.where(odd, 1.0, 0.0).astype(F32)
        row = sums[0:1] * (1.0 - mine) + sums[1:2] * mine
        level = lax.broadcasted_iota(jnp.int32, (8, TOKC), 0)
        tile[1] = tile[1] + jnp.where(level == 1, row, 0.0)

    reduce_start(1)
    gate((jnp.logical_and(z == 0, y == 1), lambda: loop(HEADS, finish)))
    total = reduce_finish(1)
    query_inner = to_full(total[0:1]) * inv[0] * inv[0] * inv[0] / D
    inv[2] = to_full(total[1:2]) * inv[1] * inv[1] * inv[1] / D
    for h in range(HEADS):
        at = pl.ds(h * HDIM, HDIM)
        dq_out[:, at] = (dq[h] * gain(0, h) * inv[0] - qd[h, 1].astype(F32) * query_inner).astype(BF16)

    gate((owner, lambda: loop(HEADS, finish)))

    for h in range(HEADS):
        at = pl.ds(h * HDIM, HDIM)
        dk_out[:, at] = (dk[h] * SCALE * gain(1, h) * inv[1] - kv[h, 1].astype(F32) * inv[2]).astype(BF16)

    @pl.when(owner)
    def _():
        for h in range(HEADS):
            value_back(h).wait_recv()
            dv[h] = dv[h] + vin[h].astype(F32)

    for h in range(HEADS):
        dv_out[:, pl.ds(h * HDIM, HDIM)] = dv[h].astype(BF16)

    def drain(h):
        gate(
            (c <= 29, kv_own(h).wait_send), (jnp.logical_or(even, kv_on), kv_beside(h).wait_send),
            (kv_has, kv_across(h).wait_send), (c >= 2, qd_own(h).wait_send),
            (jnp.logical_or(odd, qd_on), qd_beside(h).wait_send), (qd_has, qd_across(h).wait_send),
            (has_mate, mate_copy(h).wait_send),
        )
        each_kid(lambda i, kid: kid_copy(i, kid, h).wait_send())
        chip_copy(h).wait_send()
        relay_copy(h).wait_send()
        for i in (1, 2, 3):
            partial_copy(i, h).wait_send()
            stat_copy(i, h).wait_send()
        each_parent(lambda slot, parent: up_copy(slot, parent, h).wait_send())

        @pl.when(owner)
        def _():
            for i in range(len(VALUE_KIDS)):
                value_copy(i, h).wait_send()

        @pl.when(jnp.logical_and(z == 0, y == 1))
        def _():
            value_back(h).wait_send()

    loop(HEADS, drain)

    @pl.when(owner)
    def _():
        each_other(lambda i: inverse_copy(i).wait_send())

    for root in (0, 1):
        @pl.when(c != root)
        def _():
            tile_copy(root).wait_send()

    for i in range(len(NEAR)):
        near_copy(i).wait_send()
    for phase in (0, 1):
        for shift in range(1, HEAD_DEVICES):
            reduce_copy(phase, shift).wait_send()


def hand_on(*refs):
    held, sem = refs[8:]
    reads = [pltpu.make_async_copy(refs[i], held.at[i], sem.at[0, i]) for i in range(4)]
    writes = [pltpu.make_async_copy(held.at[i], refs[4 + i], sem.at[1, i]) for i in range(4)]
    for read in reads:
        read.start()
    for read, write in zip(reads, writes):
        read.wait()
        write.start()
    for write in writes:
        write.wait()


def per_device(query_raw, key_raw, values, query_gain, key_gain, recent_ids, sink_ids, out_grad):
    rows, width = query_raw.shape
    block = (HEADS, TOKC, HDIM)
    pair = (HEADS, 2, TOKC, HDIM)
    dma = pltpu.SemaphoreType.DMA
    any_spec = pl.BlockSpec(memory_space=pltpu.HBM)
    vmem = pl.BlockSpec(memory_space=pltpu.VMEM)
    smem = pl.BlockSpec(memory_space=pltpu.SMEM)
    outputs = pl.pallas_call(
        kernel,
        out_shape=[jax.ShapeDtypeStruct((rows, width), BF16)] * 4,
        in_specs=[any_spec] * 6 + [smem] * 2,
        out_specs=[vmem] * 4,
        scratch_shapes=[
            pltpu.VMEM(pair, BF16),
            pltpu.VMEM(pair, BF16),
            pltpu.VMEM(block, BF16),
            pltpu.VMEM(block, BF16),
            pltpu.VMEM((3,) + pair, BF16),
            pltpu.VMEM((3,) + pair, BF16),
            pltpu.VMEM((2, 2) + block, BF16),
            pltpu.VMEM((2, 2) + block, BF16),
            pltpu.VMEM((3,) + block, BF16),
            pltpu.VMEM((3,) + block, BF16),
            pltpu.VMEM(block, F32),
            pltpu.VMEM(block, BF16),
            pltpu.VMEM(block, BF16),
            pltpu.VMEM(block, F32),
            pltpu.VMEM(block, F32),
            pltpu.VMEM(block, F32),
            pltpu.VMEM((HEADS, 8, TOKC), F32),
            pltpu.VMEM((3, HEADS, 8, TOKC), F32),
            pltpu.VMEM((2, 8, TOKC), F32),
            pltpu.VMEM((2, HEAD_DEVICES - 1, 8, TOKC), F32),
            pltpu.VMEM((8, TOKC, HDIM), F32),
            pltpu.VMEM((2, width), F32),
            pltpu.VMEM((3, 8, TOKC), F32),
            pltpu.VMEM((len(NEAR), 8, TOKC), F32),
            pltpu.VMEM((TOKC, HDIM), F32),
            pltpu.VMEM((8, TOKC), F32),
            pltpu.VMEM((STRETCHES, 8, TOKC), F32),
            dma((4, HEADS)),
            dma((2,)),
            dma((3, HEADS)),
            dma((3, HEADS)),
            dma((3, HEADS)),
            dma((3, HEADS)),
            dma((3, HEADS)),
            dma((3, HEADS)),
            dma((2, 2, HEADS)),
            dma((3, HEADS)),
            dma((3, HEADS)),
            dma((2, HEAD_DEVICES - 1)),
            dma((2, HEAD_DEVICES - 1)),
            dma((3, HEADS)),
            dma((3, HEADS)),
            dma((HEADS,)),
            dma((3, HEADS)),
            dma((HEADS,)),
            dma((HEADS,)),
            dma((len(VALUE_KIDS), HEADS)),
            dma((STRETCHES,)),
            dma((2,)),
            dma((2,)),
            dma((STRETCHES,)),
            dma((len(NEAR),)),
            dma((len(NEAR),)),
        ],
        compiler_params=pltpu.CompilerParams(
            collective_id=0, has_side_effects=True, vmem_limit_bytes=60 * 2**20
        ),
        cost_estimate=pl.CostEstimate(flops=3 * 10**9, bytes_accessed=6 * 10**6, transcendentals=3 * 10**6),
        name="stretch_attention",
    )(
        query_raw, key_raw, values, out_grad, query_gain, key_gain, recent_ids, sink_ids,
    )
    return pl.pallas_call(
        hand_on,
        out_shape=[jax.ShapeDtypeStruct((rows, width), BF16)] * 4,
        in_specs=[any_spec] * 4,
        out_specs=[any_spec] * 4,
        scratch_shapes=[pltpu.VMEM((4, rows, width), BF16), dma((2, 4))],
        name="hand_on",
    )(*outputs)


def solution(mesh):
    split = P("stretch", "head")
    return jax.shard_map(
        per_device,
        mesh=mesh,
        in_specs=(split, split, split, P("head"), P("head"), P("stretch", None), P("stretch", None), split),
        out_specs=(split,) * 4,
        check_vma=False,
    )
```
